256 devices in a mesh: row: 8 (over z), col: 8 (over y, core), depth: 4 (over x).
Axes of the slice: x: 4, y: 4, z: 8, core: 2. Of those that a mesh axis runs over, the one named last changes fastest.
Arguments:
- features: bfloat16 [512, 6144], P(('col', 'depth'), 'row')
- cotangent: bfloat16 [512, 6144], P(('col', 'depth'), 'row')
- gate_master: float32 [6144, 24576], P('row', ('col', 'depth'))
- up_master: float32 [6144, 24576], P('row', ('col', 'depth'))
- down_master: float32 [24576, 6144], P(('col', 'depth'), 'row')
Outputs:
- gate_gradient: bfloat16 [6144, 24576], P('row', ('col', 'depth'))
- up_gradient: bfloat16 [6144, 24576], P('row', ('col', 'depth'))
- down_gradient: bfloat16 [24576, 6144], P(('col', 'depth'), 'row')
All inputs are finite; a program needn't handle non-finite values.
Results may differ from the reference program's by a relative error of at most 0.0075.
Values may be sent and summed in bfloat16 or wider, within the bound.
A program may use at most 64 MiB of HBM per device.

```python
import math
import jax
import jax.numpy as jnp
from jax import lax

D = 6144
FF = 24576
TOKENS = 512


def rising_profile(key, length, spread):
    log_level = jax.random.uniform(key, (length,), jnp.float32, -spread, spread)
    trend_line = 1.0 + 2.0 * jnp.arange(length, dtype=jnp.float32) / length
    energy = math.sinh(2.0 * spread) / (2.0 * spread) * 13.0 / 3.0
    return jnp.exp(log_level) * trend_line / math.sqrt(energy)


def flat_profile(key, length, spread):
    log_level = jax.random.uniform(key, (length,), jnp.float32, -spread, spread)
    energy = math.sinh(2.0 * spread) / (2.0 * spread)
    return jnp.exp(log_level) / math.sqrt(energy)


def draw_features(key, part):
    key = jax.random.fold_in(key, 11)
    base_key, side_key = jax.random.split(key)
    base = jnp.clip(jax.random.normal(base_key, (TOKENS, D), jnp.float32), -5.0, 5.0)
    spread = 1.15
    return (base * rising_profile(side_key, D, spread)[None, :]).astype(jnp.bfloat16)


def draw_cotangent(key, part):
    key = jax.random.fold_in(key, 23)
    base_key, side_key = jax.random.split(key)
    base = jnp.clip(jax.random.normal(base_key, (TOKENS, D), jnp.float32), -5.0, 5.0)
    spread = 1.15
    factor = 1.0 / math.sqrt(TOKENS)
    return (base * rising_profile(side_key, D, spread)[None, :] * factor).astype(jnp.bfloat16)


def draw_gate_master(key, part):
    key = jax.random.fold_in(key, 37)
    base_key, row_key, column_key = jax.random.split(key, 3)
    base = jnp.clip(jax.random.normal(base_key, (D, FF), jnp.float32), -5.0, 5.0)
    spread = 1.15
    factor = 1.0 / math.sqrt(D)
    return base * rising_profile(row_key, D, spread)[:, None] * flat_profile(column_key, FF, spread)[None, :] * factor


def draw_up_master(key, part):
    key = jax.random.fold_in(key, 41)
    base_key, row_key, column_key = jax.random.split(key, 3)
    base = jnp.clip(jax.random.normal(base_key, (D, FF), jnp.float32), -5.0, 5.0)
    spread = 1.15
    factor = 1.0 / math.sqrt(D)
    return base * rising_profile(row_key, D, spread)[:, None] * flat_profile(column_key, FF, spread)[None, :] * factor


def draw_down_master(key, part):
    key = jax.random.fold_in(key, 53)
    base_key, row_key, column_key = jax.random.split(key, 3)
    base = jnp.clip(jax.random.normal(base_key, (FF, D), jnp.float32), -5.0, 5.0)
    spread = 1.15
    factor = 1.0 / math.sqrt(FF)
    return base * flat_profile(row_key, FF, spread)[:, None] * rising_profile(column_key, D, spread)[None, :] * factor


def setup_inputs(seed: int = 0) -> dict:
    arg_keys = jax.random.split(jax.random.key(seed), 6)
    features = draw_features(jax.random.fold_in(arg_keys[5], 71), 0)
    cotangent = draw_cotangent(jax.random.fold_in(arg_keys[5], 71), 0)
    gate_master = draw_gate_master(jax.random.fold_in(arg_keys[5], 71), 0)
    up_master = draw_up_master(jax.random.fold_in(arg_keys[5], 71), 0)
    down_master = draw_down_master(jax.random.fold_in(arg_keys[5], 71), 0)
    return dict(features=features, cotangent=cotangent, gate_master=gate_master, up_master=up_master, down_master=down_master)


radius = 0.3

def pointwise(gate_sum, up_sum, back_sum):
    sigmoid_gate = jax.nn.sigmoid(gate_sum)
    swish_gate = gate_sum * sigmoid_gate
    activation = (swish_gate * up_sum).astype(jnp.bfloat16)
    gate_delta = (back_sum * up_sum * sigmoid_gate * (1.0 + gate_sum * (1.0 - sigmoid_gate))).astype(jnp.bfloat16)
    up_delta = (back_sum * swish_gate).astype(jnp.bfloat16)
    return (activation, gate_delta, up_delta)

def pass_gradients(features, cotangent, gate_weight, up_weight, down_weight):
    contract = (((0,), (0,)), ((), ()))
    gate_sum = jnp.dot(features, gate_weight, preferred_element_type=jnp.float32)
    up_sum = jnp.dot(features, up_weight, preferred_element_type=jnp.float32)
    back_sum = lax.dot_general(cotangent, down_weight, (((1,), (1,)), ((), ())), preferred_element_type=jnp.float32)
    activation, gate_delta, up_delta = pointwise(gate_sum, up_sum, back_sum)
    gate_grad = lax.dot_general(features, gate_delta, contract, preferred_element_type=jnp.float32)
    up_grad = lax.dot_general(features, up_delta, contract, preferred_element_type=jnp.float32)
    down_grad = lax.dot_general(activation, cotangent, contract, preferred_element_type=jnp.float32)
    return (gate_grad, up_grad, down_grad)

def reference(features, cotangent, gate_master, up_master, down_master):
    first_gate, first_up, first_down = pass_gradients(features, cotangent, gate_master.astype(jnp.bfloat16), up_master.astype(jnp.bfloat16), down_master.astype(jnp.bfloat16))
    weight_energy = jnp.sum(gate_master * gate_master) + jnp.sum(up_master * up_master) + jnp.sum(down_master * down_master)
    gradient_energy = jnp.sum(first_gate * first_gate) + jnp.sum(first_up * first_up) + jnp.sum(first_down * first_down)
    step_scale = radius * jnp.sqrt(weight_energy) / jnp.sqrt(gradient_energy + 1e-06)
    perturbed_gate = (gate_master + step_scale * first_gate).astype(jnp.bfloat16)
    perturbed_up = (up_master + step_scale * first_up).astype(jnp.bfloat16)
    perturbed_down = (down_master + step_scale * first_down).astype(jnp.bfloat16)
    gate_grad, up_grad, down_grad = pass_gradients(features, cotangent, perturbed_gate, perturbed_up, perturbed_down)
    return (gate_grad.astype(jnp.bfloat16), up_grad.astype(jnp.bfloat16), down_grad.astype(jnp.bfloat16))
```

```python
import jax
import jax.numpy as jnp
from jax import lax
from jax.sharding import PartitionSpec as P

radius = 0.3
ROW_CONTRACT = (((1,), (1,)), ((), ()))


def pointwise(gate_sum, up_sum, back_sum):
    sigmoid_gate = jax.nn.sigmoid(gate_sum)
    swish_gate = gate_sum * sigmoid_gate
    activation = (swish_gate * up_sum).astype(jnp.bfloat16)
    gate_delta = (
        back_sum * up_sum * sigmoid_gate * (1.0 + gate_sum * (1.0 - sigmoid_gate))
    ).astype(jnp.bfloat16)
    up_delta = (back_sum * swish_gate).astype(jnp.bfloat16)
    return (activation, gate_delta, up_delta)


def split_dot(delta, gram):
    high = gram.astype(jnp.bfloat16)
    low = (gram - high.astype(jnp.float32)).astype(jnp.bfloat16)
    return jnp.dot(delta, high, preferred_element_type=jnp.float32) + jnp.dot(
        delta, low, preferred_element_type=jnp.float32
    )


def shards(features, cotangent, gate_master, up_master, down_master):
    tokens_all, targets_all = (
        lax.all_gather(features, ("col", "depth"), axis=0, tiled=True),
        lax.all_gather(cotangent, ("col", "depth"), axis=0, tiled=True),
    )
    gram_rows = jnp.concatenate(
        [
            lax.dot_general(features, tokens_all, ROW_CONTRACT, preferred_element_type=jnp.float32),
            lax.dot_general(cotangent, targets_all, ROW_CONTRACT, preferred_element_type=jnp.float32),
        ],
        axis=1,
    )
    gram_all = lax.all_gather(
        lax.psum(gram_rows, "row"), ("col", "depth"), axis=0, tiled=True
    )
    tokens_gram, targets_gram = jnp.split(gram_all, 2, axis=1)

    first_contract = (((0,), (1,)), ((), ()))
    gate_weight, up_weight, down_weight = (
        gate_master.astype(jnp.bfloat16),
        up_master.astype(jnp.bfloat16),
        down_master.astype(jnp.bfloat16),
    )
    partial_sums = jnp.stack(
        [
            lax.dot_general(gate_weight, tokens_all, first_contract, preferred_element_type=jnp.float32),
            lax.dot_general(up_weight, tokens_all, first_contract, preferred_element_type=jnp.float32),
            lax.dot_general(down_weight, targets_all, ROW_CONTRACT, preferred_element_type=jnp.float32),
        ]
    )
    sums = lax.psum_scatter(partial_sums, "row", scatter_dimension=1, tiled=True)
    gate_sum, up_sum, back_sum = sums[0], sums[1], sums[2]
    activation, gate_delta, up_delta = pointwise(gate_sum, up_sum, back_sum)
    gate_step = split_dot(gate_delta, tokens_gram)
    up_step = split_dot(up_delta, tokens_gram)
    back_step = split_dot(activation, targets_gram)
    weight_local = (
        jnp.sum(gate_master * gate_master)
        + jnp.sum(up_master * up_master)
        + jnp.sum(down_master * down_master)
    )
    gradient_local = (
        jnp.sum(gate_delta.astype(jnp.float32) * gate_step)
        + jnp.sum(up_delta.astype(jnp.float32) * up_step)
        + jnp.sum(activation.astype(jnp.float32) * back_step)
    )
    weight_energy, gradient_energy = lax.psum(
        (weight_local, gradient_local), ("row", "col", "depth")
    )
    step_scale = radius * jnp.sqrt(weight_energy) / jnp.sqrt(gradient_energy + 1e-06)
    second = jnp.stack(
        pointwise(
            gate_sum + step_scale * gate_step,
            up_sum + step_scale * up_step,
            back_sum + step_scale * back_step,
        )
    )
    second_all = lax.all_gather(second, "row", axis=1, tiled=True)
    last_contract = (((0,), (1,)), ((), ()))
    gate_grad = lax.dot_general(
        tokens_all, second_all[1], last_contract, preferred_element_type=jnp.float32
    )
    up_grad = lax.dot_general(
        tokens_all, second_all[2], last_contract, preferred_element_type=jnp.float32
    )
    down_grad = jnp.dot(second_all[0], targets_all, preferred_element_type=jnp.float32)
    return (
        gate_grad.astype(jnp.bfloat16),
        up_grad.astype(jnp.bfloat16),
        down_grad.astype(jnp.bfloat16),
    )


def solution(mesh):
    placed = (
        P(("col", "depth"), "row"),
        P(("col", "depth"), "row"),
        P("row", ("col", "depth")),
        P("row", ("col", "depth")),
        P(("col", "depth"), "row"),
    )
    return jax.shard_map(
        shards,
        mesh=mesh,
        in_specs=placed,
        out_specs=(
            P("row", ("col", "depth")),
            P("row", ("col", "depth")),
            P(("col", "depth"), "row"),
        ),
        check_vma=False,
    )
```

```python
import functools

import jax
import jax.numpy as jnp
from jax import lax
from jax.experimental import pallas as pl
from jax.experimental.pallas import tpu as pltpu
from jax.sharding import PartitionSpec as P

radius = 0.3
MESH = pl.DeviceIdType.MESH
NT = (((1,), (1,)), ((), ()))
f32, bf16 = jnp.float32, jnp.bfloat16


def pointwise(gate_sum, up_sum, back_sum):
    sigmoid_gate = jax.nn.sigmoid(gate_sum)
    swish_gate = gate_sum * sigmoid_gate
    activation = (swish_gate * up_sum).astype(bf16)
    gate_delta = (
        back_sum * up_sum * sigmoid_gate * (1.0 + gate_sum * (1.0 - sigmoid_gate))
    ).astype(bf16)
    up_delta = (back_sum * swish_gate).astype(bf16)
    return (activation, gate_delta, up_delta)


def fold(x):
    rows, lanes = x.shape
    x = jnp.sum(x.reshape(rows // 8, 8, lanes), axis=0)
    return sum(x[:, i : i + 128] for i in range(0, lanes, 128))


def kernel(
    NZ, NY, NX,
    features, cotangent, gate_master, up_master, down_master,
    deltas_out, tokens_t_out, targets_out,
    tok, tgt, stage, weights, tokens_t, part, outbox, inbox,
    kpart, kin, kown, kf, kc, gram, sums, steps, deltas, energy, energy_in,
    local_sem, tok_s, tok_r, k_s, k_r, kz_s, kz_r, ch_s, ch_r, ag_s, ag_r, en_s, en_r,
):
    z, c, x = lax.axis_index("row"), lax.axis_index("col"), lax.axis_index("depth")
    y, k = c // 2, c % 2
    hidden = weights.shape[1]
    tokens = tokens_t.shape[1]
    half = part.shape[3]

    def at_z(i):
        return ((z + i + NZ) % NZ, c, x)

    def at_y(i):
        return (z, ((y + i) % NY) * 2 + k, x)

    def at_x(i):
        return (z, c, (x + i) % NX)

    sibling = (z, y * 2 + (1 - k), x)

    def remote(src, dst, ssem, rsem, device):
        return pltpu.make_async_remote_copy(
            src_ref=src, dst_ref=dst, send_sem=ssem, recv_sem=rsem,
            device_id=device, device_id_type=MESH,
        )

    def arrive(dst, ssem, rsem):
        remote(dst, dst, ssem, rsem, sibling).wait_recv()

    def leave(src, ssem, rsem):
        remote(src, src, ssem, rsem, sibling).wait_send()

    masters = (gate_master, up_master, down_master)
    loads = [pltpu.make_async_copy(masters[m], stage.at[m], local_sem.at[m]) for m in range(3)]
    for load in loads:
        load.start()

    barrier = pltpu.get_barrier_semaphore()
    partners = (
        [at_z(i) for i in range(1, NZ)]
        + [at_y(i) for i in range(1, NY)]
        + [at_x(i) for i in range(1, NX)]
        + [sibling]
    )
    for device in partners:
        pl.semaphore_signal(barrier, inc=1, device_id=device, device_id_type=MESH)
    pl.semaphore_wait(barrier, len(partners))

    def plane_first(a, b, ss, rs):
        for i in range(1, NX):
            remote(a.at[y, k, x], a.at[y, k, x], ss.at[0, 0, i], rs.at[0, 0, i], at_x(i)).start()
        for i in range(1, NY):
            remote(b.at[y, k, x], b.at[y, k, x], ss.at[1, 0, i], rs.at[1, 0, i], at_y(i)).start()

    def plane_second(a, b, ss, rs):
        for i in range(1, NX):
            arrive(a.at[y, k, (x - i + NX) % NX], ss.at[0, 0, i], rs.at[0, 0, i])
        for i in range(1, NY):
            remote(a.at[y, k], a.at[y, k], ss.at[0, 1, i], rs.at[0, 1, i], at_y(i)).start()
        for i in range(1, NY):
            arrive(b.at[(y - i + NY) % NY, k, x], ss.at[1, 0, i], rs.at[1, 0, i])
        for i in range(1, NX):
            remote(b.at[:, k, x], b.at[:, k, x], ss.at[1, 1, i], rs.at[1, 1, i], at_x(i)).start()
        remote(a.at[y, k], a.at[y, k], ss.at[0, 2, 0], rs.at[0, 2, 0], sibling).start()
        remote(b.at[:, k, x], b.at[:, k, x], ss.at[1, 2, 0], rs.at[1, 2, 0], sibling).start()

    def plane_third(a, b, ss, rs):
        for i in range(1, NY):
            part_a = a.at[(y - i + NY) % NY, k]
            arrive(part_a, ss.at[0, 1, i], rs.at[0, 1, i])
            remote(part_a, part_a, ss.at[0, 2, i], rs.at[0, 2, i], sibling).start()
        for i in range(1, NX):
            part_b = b.at[:, k, (x - i + NX) % NX]
            arrive(part_b, ss.at[1, 1, i], rs.at[1, 1, i])
            remote(part_b, part_b, ss.at[1, 2, i], rs.at[1, 2, i], sibling).start()

    def plane_last(a, b, ss, rs):
        for i in range(NY):
            arrive(a.at[(y - i + NY) % NY, 1 - k], ss.at[0, 2, i], rs.at[0, 2, i])
        for i in range(NX):
            arrive(b.at[:, 1 - k, (x - i + NX) % NX], ss.at[1, 2, i], rs.at[1, 2, i])

    def plane_leave(a, b, ss, rs):
        for i in range(1, NX):
            leave(a.at[y, k, x], ss.at[0, 0, i], rs.at[0, 0, i])
        for i in range(1, NY):
            leave(b.at[y, k, x], ss.at[1, 0, i], rs.at[1, 0, i])
        for i in range(1, NY):
            leave(a.at[y, k], ss.at[0, 1, i], rs.at[0, 1, i])
        for i in range(1, NX):
            leave(b.at[:, k, x], ss.at[1, 1, i], rs.at[1, 1, i])
        for i in range(NY):
            leave(a.at[(y - i + NY) % NY, k], ss.at[0, 2, i], rs.at[0, 2, i])
        for i in range(NX):
            leave(b.at[:, k, (x - i + NX) % NX], ss.at[1, 2, i], rs.at[1, 2, i])

    tok[y, k, x] = features[...]
    tgt[y, k, x] = cotangent[...]
    plane_first(tok, tgt, tok_s, tok_r)

    def prepare(m, transpose):
        loads[m].wait()
        rows = 128

        def body(i, total):
            r = pl.ds(pl.multiple_of(i * rows, rows), rows)
            block = stage[m, r, :]
            if transpose:
                weights[m, :, r] = block.astype(bf16).T
            else:
                weights[m, r, :] = block.astype(bf16)
            return total + fold(block * block)

        return lax.fori_loop(0, hidden // rows, body, jnp.zeros((8, 128), f32))

    weight_energy = prepare(0, True)
    plane_second(tok, tgt, tok_s, tok_r)
    weight_energy += prepare(1, True)
    plane_third(tok, tgt, tok_s, tok_r)
    weight_energy += prepare(2, False)
    plane_last(tok, tgt, tok_s, tok_r)

    for own, every, base in ((features, tok, 0), (cotangent, tgt, NZ // 2)):
        rows = lax.dot_general(
            own[...], every[...].reshape(tokens, -1), NT, preferred_element_type=f32
        )
        for j in range(NZ // 2):
            kpart[base + j] = rows[:, j * 128 : (j + 1) * 128]
    for i in range(1, NZ):
        remote(
            kpart.at[(z + i) % NZ], kin.at[i], kz_s.at[0, i], kz_r.at[0, i], at_z(i)
        ).start()

    chains = []
    for d, sign in ((0, 1), (1, -1)):
        for h in range(2):
            chains.append((d, sign, h, NZ // 2 if d == h else NZ // 2 - 1))
    chains.sort(key=lambda chain: -chain[3])

    def chain_send(t, m):
        for d, sign, h, n in chains:
            if t >= n:
                continue
            owner = (z + sign * (n - t) + NZ) % NZ
            total = part[m, owner, h]
            if t > 0:
                arrive(inbox.at[d, t - 1, m, h], ch_s.at[d, t - 1, m, h], ch_r.at[d, t - 1, m, h])
                total = total + inbox[d, t - 1, m, h].astype(f32)
            outbox[d, t, m, h] = total.astype(outbox.dtype)
            remote(
                outbox.at[d, t, m, h], inbox.at[d, t, m, h],
                ch_s.at[d, t, m, h], ch_r.at[d, t, m, h], at_z(sign),
            ).start()

    for m in range(3):
        every = tok if m < 2 else tgt
        wide = hidden // 2
        for i in range(2):
            part[m, i * (NZ // 2) : (i + 1) * (NZ // 2)] = lax.dot_general(
                weights[m, i * wide : (i + 1) * wide, :],
                every[...].reshape(tokens, -1), NT, preferred_element_type=f32,
            ).reshape(NZ // 2, 2, half, tokens)
        chain_send(0, m)

    def loop3(f):
        def body(m, carry):
            f(m)
            return carry

        lax.fori_loop(0, 3, body, 0)

    for i in range(1, NZ):
        arrive(kin.at[i], kz_s.at[0, i], kz_r.at[0, i])
    total = kpart[z]
    for i in range(1, NZ):
        total = total + kin[i]
    kown[z] = total
    for i in range(1, NZ):
        remote(kown.at[z], kown.at[z], kz_s.at[1, i], kz_r.at[1, i], at_z(i)).start()

    loop3(lambda m: chain_send(1, m))

    for i in range(1, NZ):
        arrive(kown.at[(z - i + NZ) % NZ], kz_s.at[1, i], kz_r.at[1, i])
    kf[y, k, x] = kown[0 : NZ // 2]
    kc[y, k, x] = kown[NZ // 2 : NZ]
    plane_first(kf, kc, k_s, k_r)

    tokens_t[...] = tok[...].reshape(tokens, -1).T
    copies = [
        pltpu.make_async_copy(tokens_t, tokens_t_out, local_sem.at[0]),
        pltpu.make_async_copy(tgt, targets_out, local_sem.at[1]),
    ]
    for copy in copies:
        copy.start()

    loop3(lambda m: chain_send(2, m))
    plane_second(kf, kc, k_s, k_r)
    loop3(lambda m: chain_send(3, m))
    plane_third(kf, kc, k_s, k_r)

    plane_last(kf, kc, k_s, k_r)
    for j in range(NZ // 2):
        for g, every in enumerate((kf, kc)):
            block = every[:, :, :, j].reshape(tokens, 128)
            high = block.astype(bf16)
            gram[g, 0, :, j * 128 : (j + 1) * 128] = high
            gram[g, 1, :, j * 128 : (j + 1) * 128] = (block - high.astype(f32)).astype(bf16)

    def chain_last(m):
        for h in range(2):
            total = part[m, z, h]
            for d, sign, h2, n in chains:
                if h2 != h:
                    continue
                arrive(inbox.at[d, n - 1, m, h], ch_s.at[d, n - 1, m, h], ch_r.at[d, n - 1, m, h])
                total = total + inbox[d, n - 1, m, h].astype(f32)
            sums[m, h] = total

    loop3(chain_last)

    own = 2 * half
    gate_sum, up_sum, back_sum = (sums[m].reshape(own, tokens) for m in range(3))
    activation, gate_delta, up_delta = pointwise(gate_sum, up_sum, back_sum)

    def gram_dot(delta, g):
        return jnp.dot(delta, gram[g, 0], preferred_element_type=f32) + jnp.dot(
            delta, gram[g, 1], preferred_element_type=f32
        )

    both = gram_dot(jnp.concatenate([gate_delta, up_delta], axis=0), 0)
    back_step = gram_dot(activation, 1)
    gate_step, up_step = both[:own], both[own:]
    steps[0], steps[1], steps[2] = gate_step, up_step, back_step
    gradient_energy = (
        fold(gate_delta.astype(f32) * gate_step)
        + fold(up_delta.astype(f32) * up_step)
        + fold(activation.astype(f32) * back_step)
    )
    both_energy = jnp.concatenate(
        [
            jnp.sum(weight_energy, axis=0, keepdims=True),
            jnp.sum(gradient_energy, axis=0, keepdims=True),
            jnp.zeros((6, 128), f32),
        ],
        axis=0,
    )
    for axis, (count, where) in enumerate(
        ((NX, at_x), (NY, at_y), (2, lambda i: sibling), (NZ, at_z))
    ):
        energy[axis] = both_energy
        for i in range(1, count):
            remote(
                energy.at[axis], energy_in.at[axis, i], en_s.at[axis, i], en_r.at[axis, i], where(i)
            ).start()
        for i in range(1, count):
            arrive(energy_in.at[axis, i], en_s.at[axis, i], en_r.at[axis, i])
            both_energy = both_energy + energy_in[axis, i]
    totals = jnp.sum(both_energy, axis=1, keepdims=True)
    step_scale = (
        radius * jnp.sqrt(totals[0:1]) / jnp.sqrt(jnp.maximum(totals[1:2], 0.0) + 1e-06)
    )

    second = pointwise(
        sums[0].reshape(own, tokens) + step_scale * steps[0],
        sums[1].reshape(own, tokens) + step_scale * steps[1],
        sums[2].reshape(own, tokens) + step_scale * steps[2],
    )

    def spread(t, m):
        for d, sign, h, n in chains:
            owner = (z - sign * t + NZ) % NZ
            block = deltas.at[m, owner, h]
            if 0 < t <= n:
                arrive(block, ag_s.at[d, t - 1, m, h], ag_r.at[d, t - 1, m, h])
            if t < n:
                remote(
                    block, block, ag_s.at[d, t, m, h], ag_r.at[d, t, m, h], at_z(sign)
                ).start()

    for m in range(3):
        deltas[m, z] = second[m].reshape(2, half, tokens)
        spread(0, m)
    for t in range(1, NZ // 2 + 1):
        loop3(functools.partial(spread, t))
    last = pltpu.make_async_copy(deltas, deltas_out, local_sem.at[2])
    last.start()

    plane_leave(tok, tgt, tok_s, tok_r)
    plane_leave(kf, kc, k_s, k_r)
    for i in range(1, NZ):
        leave(kpart.at[(z + i) % NZ], kz_s.at[0, i], kz_r.at[0, i])
        leave(kown.at[z], kz_s.at[1, i], kz_r.at[1, i])
    for axis, count in enumerate((NX, NY, 2, NZ)):
        for i in range(1, count):
            leave(energy.at[axis], en_s.at[axis, i], en_r.at[axis, i])

    def chains_leave(m):
        for d, sign, h, n in chains:
            for t in range(n):
                leave(outbox.at[d, t, m, h], ch_s.at[d, t, m, h], ch_r.at[d, t, m, h])
                leave(deltas.at[m, (z - sign * t + NZ) % NZ, h], ag_s.at[d, t, m, h], ag_r.at[d, t, m, h])

    loop3(chains_leave)
    for copy in copies:
        copy.wait()
    last.wait()


def shards(NZ, NY, NX, features, cotangent, gate_master, up_master, down_master):
    block, depth = features.shape
    hidden = gate_master.shape[1]
    tokens = block * NY * 2 * NX
    half = hidden // NZ // 2
    hops = NZ // 2
    vmem = pltpu.VMEM
    dma = pltpu.SemaphoreType.DMA
    plane = (NY, 2, NX)
    scratch = [
        vmem(plane + (block, depth), bf16),
        vmem(plane + (block, depth), bf16),
        vmem((3, depth, hidden), f32),
        vmem((3, hidden, depth), bf16),
        vmem((depth, tokens), bf16),
        vmem((3, NZ, 2, half, tokens), f32),
        vmem((2, hops, 3, 2, half, tokens), bf16),
        vmem((2, hops, 3, 2, half, tokens), bf16),
        vmem((NZ, block, 128), f32),
        vmem((NZ, block, 128), f32),
        vmem((NZ, block, 128), f32),
        vmem(plane + (NZ // 2, block, 128), f32),
        vmem(plane + (NZ // 2, block, 128), f32),
        vmem((2, 2, tokens, tokens), bf16),
        vmem((3, 2, half, tokens), f32),
        vmem((3, 2 * half, tokens), f32),
        vmem((3, NZ, 2, half, tokens), bf16),
        vmem((4, 8, 128), f32),
        vmem((4, NZ, 8, 128), f32),
        dma((3,)),
        dma((2, 3, NX)),
        dma((2, 3, NX)),
        dma((2, 3, NX)),
        dma((2, 3, NX)),
        dma((2, NZ)),
        dma((2, NZ)),
        dma((2, hops, 3, 2)),
        dma((2, hops, 3, 2)),
        dma((2, hops, 3, 2)),
        dma((2, hops, 3, 2)),
        dma((4, NZ)),
        dma((4, NZ)),
    ]
    whole = pl.BlockSpec(memory_space=vmem)
    away = pl.BlockSpec(memory_space=pl.ANY)
    deltas, tokens_t, targets = pl.pallas_call(
        functools.partial(kernel, NZ, NY, NX),
        out_shape=(
            jax.ShapeDtypeStruct((3, NZ, 2, half, tokens), bf16),
            jax.ShapeDtypeStruct((depth, tokens), bf16),
            jax.ShapeDtypeStruct(plane + (block, depth), bf16),
        ),
        in_specs=[whole, whole, away, away, away],
        out_specs=(away, away, away),
        scratch_shapes=scratch,
        compiler_params=pltpu.CompilerParams(
            collective_id=0, has_side_effects=True, vmem_limit_bytes=56 * 1024 * 1024
        ),
        cost_estimate=pl.CostEstimate(
            flops=2 * 3 * hidden * depth * tokens,
            bytes_accessed=4 * 3 * hidden * depth,
            transcendentals=0,
        ),
    )(features, cotangent, gate_master, up_master, down_master)
    deltas = deltas.reshape(3, hidden, tokens)
    targets = targets.reshape(tokens, depth)
    gate_grad = lax.dot_general(tokens_t, deltas[1], NT, preferred_element_type=f32)
    up_grad = lax.dot_general(tokens_t, deltas[2], NT, preferred_element_type=f32)
    down_grad = jnp.dot(deltas[0], targets, preferred_element_type=f32)
    return (gate_grad.astype(bf16), up_grad.astype(bf16), down_grad.astype(bf16))


def solution(mesh):
    placed = (
        P(("col", "depth"), "row"),
        P(("col", "depth"), "row"),
        P("row", ("col", "depth")),
        P("row", ("col", "depth")),
        P(("col", "depth"), "row"),
    )
    return jax.shard_map(
        functools.partial(shards, mesh.shape["row"], mesh.shape["col"] // 2, mesh.shape["depth"]),
        mesh=mesh,
        in_specs=placed,
        out_specs=(
            P("row", ("col", "depth")),
            P("row", ("col", "depth")),
            P(("col", "depth"), "row"),
        ),
        check_vma=False,
    )
```

```python
import functools

import jax
import jax.numpy as jnp
from jax import lax
from jax.experimental import pallas as pl
from jax.experimental.pallas import tpu as pltpu
from jax.sharding import PartitionSpec as P

radius = 0.3
MESH = pl.DeviceIdType.MESH
NT = (((1,), (1,)), ((), ()))
f32, bf16 = jnp.float32, jnp.bfloat16


def pointwise(gate_sum, up_sum, back_sum):
    sigmoid_gate = jax.nn.sigmoid(gate_sum)
    swish_gate = gate_sum * sigmoid_gate
    activation = (swish_gate * up_sum).astype(bf16)
    gate_delta = (
        back_sum * up_sum * sigmoid_gate * (1.0 + gate_sum * (1.0 - sigmoid_gate))
    ).astype(bf16)
    up_delta = (back_sum * swish_gate).astype(bf16)
    return (activation, gate_delta, up_delta)


def fold(x):
    rows, lanes = x.shape
    x = jnp.sum(x.reshape(rows // 8, 8, lanes), axis=0)
    return sum(x[:, i : i + 128] for i in range(0, lanes, 128))


def all_gather_plane(NY, NX, y, k, x, at_x, at_y, sibling, remote, arrive, leave):
    every = slice(None)

    def flow_parts(order):
        if order == "xy":
            first, second = at_x, at_y
            own, line = (y, k, x), (y, k, every)
            one = lambda i: (y, k, (x - i + NX) % NX)
            lines = lambda i, core: ((y - i + NY) % NY, core, every)
            return NX, NY, first, second, own, line, one, lines
        own, line = (y, k, x), (every, k, x)
        one = lambda i: ((y - i + NY) % NY, k, x)
        lines = lambda i, core: (every, core, (x - i + NX) % NX)
        return NY, NX, at_y, at_x, own, line, one, lines

    def start(flow):
        view, order, ss, rs = flow
        n1, n2, first, second, own, line, one, lines = flow_parts(order)
        for i in range(1, n1):
            remote(view(own), view(own), ss.at[0, i], rs.at[0, i], first(i)).start()

    def middle(flow):
        view, order, ss, rs = flow
        n1, n2, first, second, own, line, one, lines = flow_parts(order)
        for i in range(1, n1):
            arrive(view(one(i)), ss.at[0, i], rs.at[0, i])
        for i in range(1, n2):
            remote(view(line), view(line), ss.at[1, i], rs.at[1, i], second(i)).start()
        remote(view(line), view(line), ss.at[2, 0], rs.at[2, 0], sibling).start()

    def across(flow):
        view, order, ss, rs = flow
        n1, n2, first, second, own, line, one, lines = flow_parts(order)
        for i in range(1, n2):
            there = view(lines(i, k))
            arrive(there, ss.at[1, i], rs.at[1, i])
            remote(there, there, ss.at[2, i], rs.at[2, i], sibling).start()

    def finish(flow):
        view, order, ss, rs = flow
        n1, n2, first, second, own, line, one, lines = flow_parts(order)
        for i in range(n2):
            arrive(view(lines(i, 1 - k)), ss.at[2, i], rs.at[2, i])

    def sent(flow):
        view, order, ss, rs = flow
        n1, n2, first, second, own, line, one, lines = flow_parts(order)
        for i in range(1, n1):
            leave(view(own), ss.at[0, i], rs.at[0, i])
        for i in range(1, n2):
            leave(view(line), ss.at[1, i], rs.at[1, i])
        for i in range(n2):
            leave(view(lines(i, k)), ss.at[2, i], rs.at[2, i])

    return start, middle, across, finish, sent


def powers(largest):
    scale = jnp.ones_like(largest)
    inverse = jnp.ones_like(largest)
    for e in (64, 32, 16, 8):
        over = largest >= 2.0**e
        under = largest < 2.0**-e
        down = jnp.where(over, 2.0**-e, jnp.where(under, 2.0**e, 1.0))
        up = jnp.where(over, 2.0**e, jnp.where(under, 2.0**-e, 1.0))
        largest, scale, inverse = largest * down, scale * down, inverse * up
    return scale, inverse


def kernel(
    NZ, NY, NX,
    features, cotangent, gate_master, up_master, down_master,
    deltas_out, tokens_t_out, targets_out,
    tok, tgt, stage, weights, tokens_t, part, outbox, inbox,
    peak, peak_in, kpart, kin, kown, kplane, gram, sums, steps, deltas, energy, energy_in,
    local_sem, out_sem, plane_s, plane_r, peak_s, peak_r, kz_s, kz_r, ch_s, ch_r, ag_s, ag_r, en_s, en_r,
):
    z, c, x = lax.axis_index("row"), lax.axis_index("col"), lax.axis_index("depth")
    y, k = c // 2, c % 2
    hidden = weights.shape[1]
    depth, tokens = tokens_t.shape
    half = part.shape[3]
    block = features.shape[0]
    span = tokens // 128

    def at_z(i):
        return ((z + i + NZ) % NZ, c, x)

    def at_y(i):
        return (z, ((y + i) % NY) * 2 + k, x)

    def at_x(i):
        return (z, c, (x + i) % NX)

    def at_plane(q):
        return (z, ((y + q // NX) % NY) * 2 + k, (x + q % NX) % NX)

    def at_pair(q):
        return ((z + q // 2) % NZ, y * 2 + (k + q % 2) % 2, x)

    sibling = at_pair(1)

    def remote(src, dst, ssem, rsem, device):
        return pltpu.make_async_remote_copy(
            src_ref=src, dst_ref=dst, send_sem=ssem, recv_sem=rsem,
            device_id=device, device_id_type=MESH,
        )

    def arrive(dst, ssem, rsem):
        remote(dst, dst, ssem, rsem, sibling).wait_recv()

    def leave(src, ssem, rsem):
        remote(src, src, ssem, rsem, sibling).wait_send()

    masters = (gate_master, up_master, down_master)
    loads = [pltpu.make_async_copy(masters[m], stage.at[m], local_sem.at[m]) for m in range(3)]
    for load in loads:
        load.start()

    barrier = pltpu.get_barrier_semaphore()
    partners = [at_plane(q) for q in range(1, NY * NX)] + [at_pair(q) for q in range(1, 2 * NZ)]
    for device in partners:
        pl.semaphore_signal(barrier, inc=1, device_id=device, device_id_type=MESH)
    tok[y, k, x] = features[...]
    tgt[y, k, x] = cotangent[...]
    pl.semaphore_wait(barrier, len(partners))

    start, middle, across, finish, sent = all_gather_plane(
        NY, NX, y, k, x, at_x, at_y, sibling, remote, arrive, leave
    )

    def lanes(ref, low, high):
        return lambda where: ref.at[(*where, slice(None), pl.ds(low, high - low))]

    cut = depth // 2
    flows_tok = (
        (lanes(tok, 0, cut), "xy", plane_s.at[0], plane_r.at[0]),
        (lanes(tok, cut, depth), "yx", plane_s.at[1], plane_r.at[1]),
    )
    flows_tgt = (
        (lanes(tgt, 0, cut), "xy", plane_s.at[2], plane_r.at[2]),
        (lanes(tgt, cut, depth), "yx", plane_s.at[3], plane_r.at[3]),
    )
    flows_gram = tuple(
        (lambda where, g=g: kplane.at[(g, *where)], order, plane_s.at[4 + g], plane_r.at[4 + g])
        for g, order in enumerate(("xy", "yx"))
    )

    def run(step, flows):
        for flow in flows:
            step(flow)

    def prepare(m, transpose):
        loads[m].wait()
        rows = 128

        def body(i, total):
            r = pl.ds(pl.multiple_of(i * rows, rows), rows)
            piece = stage[m, r, :]
            if transpose:
                weights[m, :, r] = piece.astype(bf16).T
            else:
                weights[m, r, :] = piece.astype(bf16)
            return total + fold(piece * piece)

        return lax.fori_loop(0, hidden // rows, body, jnp.zeros((8, 128), f32))

    chains = []
    for d, sign in ((0, 1), (1, -1)):
        for h in range(2):
            chains.append((d, sign, h, NZ // 2 if d == h else NZ // 2 - 1))
    chains.sort(key=lambda chain: -chain[3])

    def chain_send(t, m):
        for d, sign, h, n in chains:
            if t >= n:
                continue
            owner = (z + sign * (n - t) + NZ) % NZ
            total = part[m, owner, h]
            if t > 0:
                arrive(inbox.at[d, t - 1, m, h], ch_s.at[d, t - 1, m, h], ch_r.at[d, t - 1, m, h])
                total = total + inbox[d, t - 1, m, h].astype(f32)
            outbox[d, t, m, h] = total.astype(outbox.dtype)
            remote(
                outbox.at[d, t, m, h], inbox.at[d, t, m, h],
                ch_s.at[d, t, m, h], ch_r.at[d, t, m, h], at_z(sign),
            ).start()

    def multiply(m):
        every = tok if m < 2 else tgt
        wide = hidden // 2
        for i in range(2):
            part[m, i * (NZ // 2) : (i + 1) * (NZ // 2)] = lax.dot_general(
                weights[m, i * wide : (i + 1) * wide, :],
                every[...].reshape(tokens, depth), NT, preferred_element_type=f32,
            ).reshape(NZ // 2, 2, half, tokens)

    def loop3(f):
        def body(m, carry):
            f(m)
            return carry

        lax.fori_loop(0, 3, body, 0)

    def peak_send(g, every):
        largest = jnp.max(jnp.abs(every[...].reshape(tokens // 16, 16, depth)), axis=0).astype(f32)
        largest = jnp.max(largest.reshape(2, 8, depth), axis=0)
        largest = functools.reduce(
            jnp.maximum, [largest[:, i : i + 128] for i in range(0, depth, 128)]
        )
        peak[g] = largest
        for i in range(1, NZ):
            remote(peak.at[g], peak_in.at[g, i], peak_s.at[g, i], peak_r.at[g, i], at_z(i)).start()

    def gram_partial(g, own, every):
        largest = peak[g]
        for i in range(1, NZ):
            arrive(peak_in.at[g, i], peak_s.at[g, i], peak_r.at[g, i])
            largest = jnp.maximum(largest, peak_in[g, i])
        largest = jnp.max(jnp.max(largest, axis=0, keepdims=True), axis=1, keepdims=True)
        scale, inverse = powers(largest)
        scaled = (own[...].astype(f32) * scale).astype(bf16)
        rows = lax.dot_general(
            scaled, every[...].reshape(tokens, depth), NT, preferred_element_type=f32
        ) * scale
        for r in range(block // 8):
            for j in range(span):
                kpart[g, r * span + j] = rows[r * 8 : r * 8 + 8, j * 128 : j * 128 + 128]
        for i in range(1, NZ):
            remote(
                kpart.at[g, (z + i) % NZ], kin.at[g, i], kz_s.at[g, 0, i], kz_r.at[g, 0, i], at_z(i)
            ).start()
        return inverse

    def gram_reduce(g):
        total = kpart[g, z]
        for i in range(1, NZ):
            arrive(kin.at[g, i], kz_s.at[g, 0, i], kz_r.at[g, 0, i])
            total = total + kin[g, i]
        kown[g, z] = total
        for i in range(1, NZ):
            remote(
                kown.at[g, z], kown.at[g, z], kz_s.at[g, 1, i], kz_r.at[g, 1, i], at_z(i)
            ).start()

    def gram_rows(g):
        for i in range(1, NZ):
            arrive(kown.at[g, (z - i + NZ) % NZ], kz_s.at[g, 1, i], kz_r.at[g, 1, i])
        first = ((y * 2 + k) * NX + x) * block
        rows = lax.broadcasted_iota(jnp.int32, (block, 128), 0)
        columns = lax.broadcasted_iota(jnp.int32, (block, 128), 1)
        rest = []
        for j in range(span):
            piece = jnp.concatenate([kown[g, r * span + j] for r in range(block // 8)], axis=0)
            high = piece.astype(bf16)
            kplane[g, y, k, x, j] = high
            low = jnp.where(columns + j * 128 == rows + first, piece - high.astype(f32), 0.0)
            rest.append(jnp.sum(low, axis=0, keepdims=True))
        rest.append(jnp.zeros((block - span, 128), f32))
        kplane[g, y, k, x, span] = jnp.concatenate(rest, axis=0).astype(bf16)

    run(start, flows_tok)
    run(start, flows_tgt)
    weight_energy = prepare(0, True)
    run(middle, flows_tok)
    weight_energy += prepare(1, True)
    run(across, flows_tok)
    run(middle, flows_tgt)
    run(finish, flows_tok)
    peak_send(0, tok)
    multiply(0)
    chain_send(0, 0)
    run(across, flows_tgt)
    multiply(1)
    chain_send(0, 1)
    weight_energy += prepare(2, False)
    inverse_tok = gram_partial(0, features, tok)
    run(finish, flows_tgt)
    peak_send(1, tgt)
    multiply(2)
    chain_send(0, 2)
    chain_send(1, 0)
    gram_reduce(0)
    inverse_tgt = gram_partial(1, cotangent, tgt)
    chain_send(1, 1)
    gram_rows(0)
    start(flows_gram[0])
    gram_reduce(1)
    chain_send(1, 2)
    chain_send(2, 0)
    gram_rows(1)
    start(flows_gram[1])

    tokens_t[...] = tok[...].reshape(tokens, depth).T
    copies = [
        pltpu.make_async_copy(tokens_t, tokens_t_out, local_sem.at[0]),
        pltpu.make_async_copy(tgt, targets_out, local_sem.at[1]),
    ]
    for copy in copies:
        copy.start()

    middle(flows_gram[0])
    chain_send(2, 1)
    middle(flows_gram[1])
    chain_send(2, 2)
    across(flows_gram[0])
    chain_send(3, 0)
    across(flows_gram[1])
    chain_send(3, 1)
    chain_send(3, 2)

    rest = []
    for g in range(2):
        finish(flows_gram[g])
        for j in range(span):
            gram[g, :, j * 128 : (j + 1) * 128] = kplane[g, :, :, :, j].reshape(tokens, 128)
        low = kplane[g, :, :, :, span].reshape(tokens // block, block, 128)
        low = jnp.sum(low.astype(f32), axis=0)
        rest.append(jnp.concatenate([low[j : j + 1] for j in range(span)], axis=1))

    def chain_last(m):
        for h in range(2):
            total = part[m, z, h]
            for d, sign, h2, n in chains:
                if h2 != h:
                    continue
                arrive(inbox.at[d, n - 1, m, h], ch_s.at[d, n - 1, m, h], ch_r.at[d, n - 1, m, h])
                total = total + inbox[d, n - 1, m, h].astype(f32)
            sums[m, h] = total

    loop3(chain_last)

    own = 2 * half
    gate_sum, up_sum, back_sum = (sums[m].reshape(own, tokens) for m in range(3))
    activation, gate_delta, up_delta = pointwise(gate_sum, up_sum, back_sum)

    def gram_dot(delta, g, inverse):
        product = jnp.dot(delta, gram[g], preferred_element_type=f32)
        return (product + delta.astype(f32) * rest[g]) * inverse

    both = gram_dot(jnp.concatenate([gate_delta, up_delta], axis=0), 0, inverse_tok)
    back_step = gram_dot(activation, 1, inverse_tgt)
    gate_step, up_step = both[:own], both[own:]
    steps[0], steps[1], steps[2] = gate_step, up_step, back_step
    gradient_energy = (
        fold(gate_delta.astype(f32) * inverse_tok * gate_step)
        + fold(up_delta.astype(f32) * inverse_tok * up_step)
        + fold(activation.astype(f32) * inverse_tgt * back_step)
    )
    both_energy = jnp.concatenate(
        [
            jnp.sum(weight_energy, axis=0, keepdims=True),
            jnp.sum(gradient_energy, axis=0, keepdims=True),
            jnp.zeros((6, 128), f32),
        ],
        axis=0,
    )
    spans = ((NY * NX, at_plane), (2 * NZ, at_pair))
    for axis, (count, where) in enumerate(spans):
        energy[axis] = both_energy
        for q in range(1, count):
            remote(
                energy.at[axis], energy_in.at[axis, q], en_s.at[axis, q], en_r.at[axis, q], where(q)
            ).start()
        for q in range(1, count):
            arrive(energy_in.at[axis, q], en_s.at[axis, q], en_r.at[axis, q])
            both_energy = both_energy + energy_in[axis, q]
    totals = jnp.sum(both_energy, axis=1, keepdims=True)
    step_scale = (
        radius * jnp.sqrt(totals[0:1]) / jnp.sqrt(jnp.maximum(totals[1:2], 0.0) + 1e-06)
    )
    step_tok, step_tgt = step_scale * inverse_tok, step_scale * inverse_tgt

    second = pointwise(
        sums[0].reshape(own, tokens) + step_tok * steps[0],
        sums[1].reshape(own, tokens) + step_tok * steps[1],
        sums[2].reshape(own, tokens) + step_tgt * steps[2],
    )

    def to_hbm(m, owner, h):
        return pltpu.make_async_copy(
            deltas.at[m, owner, h], deltas_out.at[m, owner, h], out_sem.at[m, owner, h]
        )

    def spread(t, m):
        for d, sign, h, n in chains:
            owner = (z - sign * t + NZ) % NZ
            there = deltas.at[m, owner, h]
            if 0 < t <= n:
                arrive(there, ag_s.at[d, t - 1, m, h], ag_r.at[d, t - 1, m, h])
            if t < n:
                remote(
                    there, there, ag_s.at[d, t, m, h], ag_r.at[d, t, m, h], at_z(sign)
                ).start()
            if 0 < t <= n:
                to_hbm(m, owner, h).start()

    for m in range(3):
        deltas[m, z] = second[m].reshape(2, half, tokens)
        spread(0, m)

    def own_to_hbm(m):
        for h in range(2):
            to_hbm(m, z, h).start()

    loop3(own_to_hbm)

    for flow in flows_tok + flows_tgt + flows_gram:
        sent(flow)
    for g in range(2):
        for i in range(1, NZ):
            leave(peak.at[g], peak_s.at[g, i], peak_r.at[g, i])
            leave(kpart.at[g, (z + i) % NZ], kz_s.at[g, 0, i], kz_r.at[g, 0, i])
            leave(kown.at[g, z], kz_s.at[g, 1, i], kz_r.at[g, 1, i])
    for axis, (count, where) in enumerate(spans):
        for q in range(1, count):
            leave(energy.at[axis], en_s.at[axis, q], en_r.at[axis, q])

    def chains_sent(m):
        for d, sign, h, n in chains:
            for t in range(n):
                leave(outbox.at[d, t, m, h], ch_s.at[d, t, m, h], ch_r.at[d, t, m, h])

    loop3(chains_sent)
    for copy in copies:
        copy.wait()

    for t in range(1, NZ // 2 + 1):
        loop3(functools.partial(spread, t))

    def spread_sent(m):
        for d, sign, h, n in chains:
            for t in range(n):
                leave(
                    deltas.at[m, (z - sign * t + NZ) % NZ, h],
                    ag_s.at[d, t, m, h], ag_r.at[d, t, m, h],
                )
        for owner in range(NZ):
            for h in range(2):
                to_hbm(m, owner, h).wait()

    loop3(spread_sent)


def gradients(tokens_t, deltas, targets, gate_out, up_out, down_out):
    gate_out[...] = lax.dot_general(
        tokens_t[...], deltas[1], NT, preferred_element_type=f32
    ).astype(bf16)
    up_out[...] = lax.dot_general(
        tokens_t[...], deltas[2], NT, preferred_element_type=f32
    ).astype(bf16)
    down_out[...] = jnp.dot(deltas[0], targets[...], preferred_element_type=f32).astype(bf16)


def shards(NZ, NY, NX, features, cotangent, gate_master, up_master, down_master):
    block, depth = features.shape
    hidden = gate_master.shape[1]
    tokens = block * NY * 2 * NX
    half = hidden // NZ // 2
    hops = NZ // 2
    span = tokens // 128
    vmem = pltpu.VMEM
    dma = pltpu.SemaphoreType.DMA
    plane = (NY, 2, NX)
    scratch = [
        vmem(plane + (block, depth), bf16),
        vmem(plane + (block, depth), bf16),
        vmem((3, depth, hidden), f32),
        vmem((3, hidden, depth), bf16),
        vmem((depth, tokens), bf16),
        vmem((3, NZ, 2, half, tokens), f32),
        vmem((2, hops, 3, 2, half, tokens), bf16),
        vmem((2, hops, 3, 2, half, tokens), bf16),
        vmem((2, 8, 128), f32),
        vmem((2, NZ, 8, 128), f32),
        vmem((2, NZ, 8, 128), f32),
        vmem((2, NZ, 8, 128), f32),
        vmem((2, NZ, 8, 128), f32),
        vmem((2,) + plane + (span + 1, block, 128), bf16),
        vmem((2, tokens, tokens), bf16),
        vmem((3, 2, half, tokens), f32),
        vmem((3, 2 * half, tokens), f32),
        vmem((3, NZ, 2, half, tokens), bf16),
        vmem((2, 8, 128), f32),
        vmem((2, NY * NX, 8, 128), f32),
        dma((3,)),
        dma((3, NZ, 2)),
        dma((6, 3, NX)),
        dma((6, 3, NX)),
        dma((2, NZ)),
        dma((2, NZ)),
        dma((2, 2, NZ)),
        dma((2, 2, NZ)),
        dma((2, hops, 3, 2)),
        dma((2, hops, 3, 2)),
        dma((2, hops, 3, 2)),
        dma((2, hops, 3, 2)),
        dma((2, NY * NX)),
        dma((2, NY * NX)),
    ]
    whole = pl.BlockSpec(memory_space=vmem)
    away = pl.BlockSpec(memory_space=pl.ANY)
    deltas, tokens_t, targets = pl.pallas_call(
        functools.partial(kernel, NZ, NY, NX),
        out_shape=(
            jax.ShapeDtypeStruct((3, NZ, 2, half, tokens), bf16),
            jax.ShapeDtypeStruct((depth, tokens), bf16),
            jax.ShapeDtypeStruct(plane + (block, depth), bf16),
        ),
        in_specs=[whole, whole, away, away, away],
        out_specs=(away, away, away),
        scratch_shapes=scratch,
        compiler_params=pltpu.CompilerParams(
            collective_id=0, has_side_effects=True, vmem_limit_bytes=56 * 1024 * 1024
        ),
        cost_estimate=pl.CostEstimate(
            flops=2 * 3 * hidden * depth * tokens,
            bytes_accessed=4 * 3 * hidden * depth,
            transcendentals=0,
        ),
    )(features, cotangent, gate_master, up_master, down_master)
    tile = hidden // 3
    return pl.pallas_call(
        gradients,
        grid=(hidden // tile,),
        out_shape=(
            jax.ShapeDtypeStruct((depth, hidden), bf16),
            jax.ShapeDtypeStruct((depth, hidden), bf16),
            jax.ShapeDtypeStruct((hidden, depth), bf16),
        ),
        in_specs=[
            pl.BlockSpec((depth, tokens), lambda i: (0, 0)),
            pl.BlockSpec((3, tile, tokens), lambda i: (0, i, 0)),
            pl.BlockSpec((tokens, depth), lambda i: (0, 0)),
        ],
        out_specs=(
            pl.BlockSpec((depth, tile), lambda i: (0, i)),
            pl.BlockSpec((depth, tile), lambda i: (0, i)),
            pl.BlockSpec((tile, depth), lambda i: (i, 0)),
        ),
        compiler_params=pltpu.CompilerParams(vmem_limit_bytes=48 * 1024 * 1024),
        cost_estimate=pl.CostEstimate(
            flops=2 * 3 * hidden * depth * tokens,
            bytes_accessed=2 * (5 * hidden * tokens + 3 * hidden * depth),
            transcendentals=0,
        ),
    )(tokens_t, deltas.reshape(3, hidden, tokens), targets.reshape(tokens, depth))


def solution(mesh):
    placed = (
        P(("col", "depth"), "row"),
        P(("col", "depth"), "row"),
        P("row", ("col", "depth")),
        P("row", ("col", "depth")),
        P(("col", "depth"), "row"),
    )
    return jax.shard_map(
        functools.partial(shards, mesh.shape["row"], mesh.shape["col"] // 2, mesh.shape["depth"]),
        mesh=mesh,
        in_specs=placed,
        out_specs=(
            P("row", ("col", "depth")),
            P("row", ("col", "depth")),
            P(("col", "depth"), "row"),
        ),
        check_vma=False,
    )
```

```python
import functools

import jax
import jax.numpy as jnp
from jax import lax
from jax.experimental import pallas as pl
from jax.experimental.pallas import tpu as pltpu
from jax.sharding import PartitionSpec as P

radius = 0.3
MESH = pl.DeviceIdType.MESH
NT = (((1,), (1,)), ((), ()))
f32, bf16 = jnp.float32, jnp.bfloat16


def pointwise(gate_sum, up_sum, back_sum):
    sigmoid_gate = jax.nn.sigmoid(gate_sum)
    swish_gate = gate_sum * sigmoid_gate
    activation = (swish_gate * up_sum).astype(bf16)
    gate_delta = (
        back_sum * up_sum * sigmoid_gate * (1.0 + gate_sum * (1.0 - sigmoid_gate))
    ).astype(bf16)
    up_delta = (back_sum * swish_gate).astype(bf16)
    return (activation, gate_delta, up_delta)


def fold(x):
    rows, lanes = x.shape
    x = jnp.sum(x.reshape(rows // 8, 8, lanes), axis=0)
    return sum(x[:, i : i + 128] for i in range(0, lanes, 128))


def all_gather_plane(NY, NX, y, x, at_x, at_y, sibling, remote, arrive, leave):
    every = slice(None)

    def parts(order):
        if order == "xy":
            return (
                NX, NY, at_x, at_y,
                lambda core: (core, y, every),
                lambda i: (0, y, (x - i + NX) % NX),
                lambda core, i: (core, (y - i + NY) % NY, every),
            )
        return (
            NY, NX, at_y, at_x,
            lambda core: (core, every, x),
            lambda i: (0, (y - i + NY) % NY, x),
            lambda core, i: (core, every, (x - i + NX) % NX),
        )

    own = (0, y, x)

    def start(flow):
        view, order, ss, rs = flow
        n1, n2, first, second, line, one, lines = parts(order)
        for i in range(1, n1):
            remote(view(own), view(own), ss.at[0, i], rs.at[0, i], first(i)).start()

    def middle(flow):
        view, order, ss, rs = flow
        n1, n2, first, second, line, one, lines = parts(order)
        for i in range(1, n1):
            arrive(view(one(i)), ss.at[0, i], rs.at[0, i])
        for i in range(1, n2):
            remote(view(line(0)), view(line(0)), ss.at[1, i], rs.at[1, i], second(i)).start()
        remote(view(line(0)), view(line(1)), ss.at[2, 0], rs.at[2, 0], sibling).start()

    def across(flow):
        view, order, ss, rs = flow
        n1, n2, first, second, line, one, lines = parts(order)
        for i in range(1, n2):
            arrive(view(lines(0, i)), ss.at[1, i], rs.at[1, i])
            remote(
                view(lines(0, i)), view(lines(1, i)), ss.at[2, i], rs.at[2, i], sibling
            ).start()

    def finish(flow):
        view, order, ss, rs = flow
        n1, n2, first, second, line, one, lines = parts(order)
        for i in range(n2):
            arrive(view(lines(1, i)), ss.at[2, i], rs.at[2, i])

    def sent(flow):
        view, order, ss, rs = flow
        n1, n2, first, second, line, one, lines = parts(order)
        for i in range(1, n1):
            leave(view(own), ss.at[0, i], rs.at[0, i])
        for i in range(1, n2):
            leave(view(line(0)), ss.at[1, i], rs.at[1, i])
        for i in range(n2):
            leave(view(lines(0, i)), ss.at[2, i], rs.at[2, i])

    return start, middle, across, finish, sent


def powers(largest):
    scale = jnp.ones_like(largest)
    inverse = jnp.ones_like(largest)
    for e in (64, 32, 16, 8):
        over = largest >= 2.0**e
        under = largest < 2.0**-e
        down = jnp.where(over, 2.0**-e, jnp.where(under, 2.0**e, 1.0))
        up = jnp.where(over, 2.0**e, jnp.where(under, 2.0**-e, 1.0))
        largest, scale, inverse = largest * down, scale * down, inverse * up
    return scale, inverse


def kernel(
    NZ, NY, NX,
    features, cotangent, gate_master, up_master, down_master,
    deltas_out, tokens_t_out, targets_out,
    tok, tgt, stage, weights, tokens_t, part, outbox, inbox,
    kpart, kin, kown, kplane, gram, sums, steps, deltas, energy, energy_in,
    local_sem, out_sem, plane_s, plane_r, kz_s, kz_r, ch_s, ch_r, ag_s, ag_r, en_s, en_r,
):
    z, c, x = lax.axis_index("row"), lax.axis_index("col"), lax.axis_index("depth")
    y, k = c // 2, c % 2
    hidden = weights.shape[1]
    depth, tokens = tokens_t.shape
    own = hidden // NZ
    half = own // 2
    side = tokens // 2
    block = features.shape[0]
    span = tokens // 128

    def at_z(i):
        return ((z + i + NZ) % NZ, c, x)

    def at_y(i):
        return (z, ((y + i) % NY) * 2 + k, x)

    def at_x(i):
        return (z, c, (x + i) % NX)

    def at_pair(q):
        return (z, ((y + q // 2) % NY) * 2 + (k + q % 2) % 2, x)

    sibling = at_pair(1)

    def remote(src, dst, ssem, rsem, device):
        return pltpu.make_async_remote_copy(
            src_ref=src, dst_ref=dst, send_sem=ssem, recv_sem=rsem,
            device_id=device, device_id_type=MESH,
        )

    def arrive(dst, ssem, rsem):
        remote(dst, dst, ssem, rsem, sibling).wait_recv()

    def leave(src, ssem, rsem):
        remote(src, src, ssem, rsem, sibling).wait_send()

    masters = (gate_master, up_master, down_master)
    loads = [pltpu.make_async_copy(masters[m], stage.at[m], local_sem.at[m]) for m in range(3)]
    loads += [
        pltpu.make_async_copy(features, tok.at[0, y, x], local_sem.at[3]),
        pltpu.make_async_copy(cotangent, tgt.at[0, y, x], local_sem.at[4]),
    ]
    for load in loads[3:] + loads[:3]:
        load.start()

    barrier = pltpu.get_barrier_semaphore()
    partners = (
        [at_x(i) for i in range(1, NX)]
        + [at_pair(q) for q in range(1, 2 * NY)]
        + [at_z(i) for i in range(1, NZ)]
    )
    for device in partners:
        pl.semaphore_signal(barrier, inc=1, device_id=device, device_id_type=MESH)
    loads[3].wait()
    loads[4].wait()
    pl.semaphore_wait(barrier, len(partners))

    start, middle, across, finish, sent = all_gather_plane(
        NY, NX, y, x, at_x, at_y, sibling, remote, arrive, leave
    )

    flows_in = (
        (lambda where: tok.at[where], "xy", plane_s.at[0], plane_r.at[0]),
        (lambda where: tgt.at[where], "yx", plane_s.at[1], plane_r.at[1]),
    )
    flows_gram = tuple(
        (lambda where, g=g: kplane.at[(g, *where)], order, plane_s.at[2 + g], plane_r.at[2 + g])
        for g, order in enumerate(("xy", "yx"))
    )

    def run(step, flows):
        for flow in flows:
            step(flow)

    def prepare(m, transpose):
        loads[m].wait()
        rows = 128

        def body(i, total):
            r = pl.ds(pl.multiple_of(i * rows, rows), rows)
            piece = stage[m, r, :]
            if transpose:
                weights[m, :, r] = piece.astype(bf16).T
            else:
                weights[m, r, :] = piece.astype(bf16)
            return total + fold(piece * piece)

        return lax.fori_loop(0, hidden // rows, body, jnp.zeros((8, 128), f32))

    def hops(d, h):
        return NZ // 2 if d == h else NZ // 2 - 1

    signs = (1, -1)

    def chain_send(t, h, m):
        for d, sign in enumerate(signs):
            n = hops(d, h)
            if t >= n:
                continue
            owner = (z + sign * (n - t) + NZ) % NZ
            total = part[h, m, owner]
            if t > 0:
                arrive(inbox.at[d, t - 1, h, m], ch_s.at[d, t - 1, h, m], ch_r.at[d, t - 1, h, m])
                total = total + inbox[d, t - 1, h, m].astype(f32)
            outbox[d, t, h, m] = total.astype(outbox.dtype)
            remote(
                outbox.at[d, t, h, m], inbox.at[d, t, h, m],
                ch_s.at[d, t, h, m], ch_r.at[d, t, h, m], at_z(sign),
            ).start()

    def multiply(h, m):
        every = tok if m < 2 else tgt
        wide = hidden // 2
        for i in range(2):
            part[h, m, i * (NZ // 2) : (i + 1) * (NZ // 2)] = lax.dot_general(
                weights[m, i * wide : (i + 1) * wide, :],
                every[h].reshape(side, depth), NT, preferred_element_type=f32,
            ).reshape(NZ // 2, own, side)

    def loop3(f):
        def body(m, carry):
            f(m)
            return carry

        lax.fori_loop(0, 3, body, 0)

    def gram_partial():
        for g, every in enumerate((tok, tgt)):
            largest = jnp.max(jnp.abs(every[...].reshape(tokens // 16, 16, depth)), axis=0)
            largest = jnp.max(largest.astype(f32), axis=0, keepdims=True)
            largest = jnp.max(largest, axis=1, keepdims=True)
            scale, inverse = powers(largest)
            scaled = (every[0, y, x].astype(f32) * scale).astype(bf16)
            rows = lax.dot_general(
                scaled, every[...].reshape(tokens, depth), NT, preferred_element_type=f32
            ) * scale
            for j in range(span):
                kpart[g * span + j, 0:block] = rows[:, j * 128 : (j + 1) * 128]
                kpart[g * span + j, block : block + 4] = jnp.broadcast_to(scale, (4, 128))
                kpart[g * span + j, block + 4 : block + 8] = jnp.broadcast_to(inverse, (4, 128))
        for i in range(1, NZ):
            remote(
                kpart.at[(z + i) % NZ], kin.at[i], kz_s.at[0, i], kz_r.at[0, i], at_z(i)
            ).start()

    def gram_reduce():
        kin[0] = kpart[z]
        for i in range(1, NZ):
            arrive(kin.at[i], kz_s.at[0, i], kz_r.at[0, i])
        scale = functools.reduce(jnp.minimum, [kin[i, block : block + 1] for i in range(NZ)])
        total = jnp.zeros((block, 128), f32)
        for i in range(NZ):
            ratio = kin[i, block + 4 : block + 5] * scale
            total = total + kin[i, 0:block] * ratio * ratio
        kown[z, 0:block] = total
        kown[z, block : block + 8] = jnp.broadcast_to(
            functools.reduce(jnp.maximum, [kin[i, block + 4 : block + 5] for i in range(NZ)]),
            (8, 128),
        )
        for i in range(1, NZ):
            remote(kown.at[z], kown.at[z], kz_s.at[1, i], kz_r.at[1, i], at_z(i)).start()

    def gram_rows():
        for i in range(1, NZ):
            arrive(kown.at[(z - i + NZ) % NZ], kz_s.at[1, i], kz_r.at[1, i])
        first = (y * NX + x) * block
        rows = lax.broadcasted_iota(jnp.int32, (block, 128), 0)
        columns = lax.broadcasted_iota(jnp.int32, (block, 128), 1)
        for g in range(2):
            rest = []
            for j in range(span):
                piece = kown[g * span + j, 0:block]
                high = piece.astype(bf16)
                kplane[g, 0, y, x, j] = high
                low = jnp.where(columns + j * 128 == rows + first, piece - high.astype(f32), 0.0)
                rest.append(jnp.sum(low, axis=0, keepdims=True))
            rest.append(jnp.zeros((block - span, 128), f32))
            kplane[g, 0, y, x, span] = jnp.concatenate(rest, axis=0).astype(bf16)

    run(start, flows_in)
    weight_energy = prepare(0, True)
    run(middle, flows_in)
    weight_energy += prepare(1, True)
    weight_energy += prepare(2, False)
    across(flows_in[0])
    for m in range(2):
        multiply(0, m)
        chain_send(0, 0, m)
    across(flows_in[1])
    multiply(0, 2)
    chain_send(0, 0, 2)
    run(finish, flows_in)
    gram_partial()
    for m in range(3):
        multiply(1, m)
    for m in range(3):
        chain_send(1, 0, m)
    gram_reduce()
    for m in range(3):
        chain_send(0, 1, m)
    for m in range(3):
        chain_send(2, 0, m)
    gram_rows()
    run(start, flows_gram)

    tokens_t[...] = tok[...].reshape(tokens, depth).T
    copies = [
        pltpu.make_async_copy(tokens_t, tokens_t_out, local_sem.at[0]),
        pltpu.make_async_copy(tgt, targets_out, local_sem.at[1]),
    ]
    for copy in copies:
        copy.start()

    for m in range(3):
        chain_send(1, 1, m)
    run(middle, flows_gram)
    for m in range(3):
        chain_send(3, 0, m)
        chain_send(2, 1, m)
    run(across, flows_gram)
    for m in range(3):
        chain_send(3, 1, m)
    run(finish, flows_gram)

    rest = []
    for g in range(2):
        low = [None] * span
        for core in range(2):
            r = slice(core * side, (core + 1) * side)
            lows = kplane[g, core, :, :, span].reshape(side // block, block, 128)
            lows = jnp.sum(lows.astype(f32), axis=0)
            for j in range(span):
                at = (j + core * span // 2) % span
                gram[g, r, at * 128 : (at + 1) * 128] = kplane[g, core, :, :, j].reshape(side, 128)
                low[at] = lows[j : j + 1] if core == 0 else low[at] + lows[j : j + 1]
        rest.append(jnp.concatenate(low, axis=1))
    inverse_tok = kown[0, block : block + 1, 0:1]
    inverse_tgt = kown[span, block : block + 1, 0:1]

    def chain_last(m):
        for h in range(2):
            total = part[h, m, z]
            for d in range(2):
                last = hops(d, h) - 1
                arrive(inbox.at[d, last, h, m], ch_s.at[d, last, h, m], ch_r.at[d, last, h, m])
                total = total + inbox[d, last, h, m].astype(f32)
            sums[m, :, h * side : (h + 1) * side] = total

    loop3(chain_last)

    gate_sum, up_sum, back_sum = sums[0], sums[1], sums[2]
    activation, gate_delta, up_delta = pointwise(gate_sum, up_sum, back_sum)

    def gram_dot(delta, g, inverse):
        product = jnp.dot(delta, gram[g], preferred_element_type=f32)
        return (product + delta.astype(f32) * rest[g]) * inverse

    both = gram_dot(jnp.concatenate([gate_delta, up_delta], axis=0), 0, inverse_tok)
    back_step = gram_dot(activation, 1, inverse_tgt)
    gate_step, up_step = both[:own], both[own:]
    steps[0], steps[1], steps[2] = gate_step, up_step, back_step
    gradient_energy = (
        fold(gate_delta.astype(f32) * inverse_tok * gate_step)
        + fold(up_delta.astype(f32) * inverse_tok * up_step)
        + fold(activation.astype(f32) * inverse_tgt * back_step)
    )
    both_energy = jnp.concatenate(
        [
            jnp.sum(weight_energy, axis=0, keepdims=True),
            jnp.sum(gradient_energy, axis=0, keepdims=True),
            jnp.zeros((6, 128), f32),
        ],
        axis=0,
    )
    spans = ((NX, at_x), (2 * NY, at_pair), (NZ, at_z))
    for axis, (count, where) in enumerate(spans):
        energy[axis] = both_energy
        for q in range(1, count):
            remote(
                energy.at[axis], energy_in.at[axis, q], en_s.at[axis, q], en_r.at[axis, q], where(q)
            ).start()
        for q in range(1, count):
            arrive(energy_in.at[axis, q], en_s.at[axis, q], en_r.at[axis, q])
            both_energy = both_energy + energy_in[axis, q]
    totals = jnp.sum(both_energy, axis=1, keepdims=True)
    step_scale = (
        radius * jnp.sqrt(totals[0:1]) / jnp.sqrt(jnp.maximum(totals[1:2], 0.0) + 1e-06)
    )
    step_tok, step_tgt = step_scale * inverse_tok, step_scale * inverse_tgt

    second = pointwise(
        sums[0] + step_tok * steps[0],
        sums[1] + step_tok * steps[1],
        sums[2] + step_tgt * steps[2],
    )

    def to_hbm(m, owner, h):
        return pltpu.make_async_copy(
            deltas.at[m, owner, h], deltas_out.at[m, owner, h], out_sem.at[m, owner, h]
        )

    def spread(t, m):
        for h in range(2):
            for d, sign in enumerate(signs):
                n = hops(d, h)
                owner = (z - sign * t + NZ) % NZ
                there = deltas.at[m, owner, h]
                if 0 < t <= n:
                    arrive(there, ag_s.at[d, t - 1, m, h], ag_r.at[d, t - 1, m, h])
                if t < n:
                    remote(
                        there, there, ag_s.at[d, t, m, h], ag_r.at[d, t, m, h], at_z(sign)
                    ).start()
                if 0 < t <= n:
                    to_hbm(m, owner, h).start()

    for m in range(3):
        deltas[m, z] = second[m].reshape(2, half, tokens)
        spread(0, m)

    def own_to_hbm(m):
        for h in range(2):
            to_hbm(m, z, h).start()

    loop3(own_to_hbm)

    for flow in flows_in + flows_gram:
        sent(flow)
    for i in range(1, NZ):
        leave(kpart.at[(z + i) % NZ], kz_s.at[0, i], kz_r.at[0, i])
        leave(kown.at[z], kz_s.at[1, i], kz_r.at[1, i])
    for axis, (count, where) in enumerate(spans):
        for q in range(1, count):
            leave(energy.at[axis], en_s.at[axis, q], en_r.at[axis, q])

    def chains_sent(m):
        for d in range(2):
            for h in range(2):
                for t in range(hops(d, h)):
                    leave(outbox.at[d, t, h, m], ch_s.at[d, t, h, m], ch_r.at[d, t, h, m])

    loop3(chains_sent)
    for copy in copies:
        copy.wait()

    for t in range(1, NZ // 2 + 1):
        loop3(functools.partial(spread, t))

    def spread_sent(m):
        for d, sign in enumerate(signs):
            for h in range(2):
                for t in range(hops(d, h)):
                    leave(
                        deltas.at[m, (z - sign * t + NZ) % NZ, h],
                        ag_s.at[d, t, m, h], ag_r.at[d, t, m, h],
                    )
        for owner in range(NZ):
            for h in range(2):
                to_hbm(m, owner, h).wait()

    loop3(spread_sent)


def gradients(tokens_t, deltas, targets, gate_out, up_out, down_out):
    gate_out[...] = lax.dot_general(
        tokens_t[...], deltas[1], NT, preferred_element_type=f32
    ).astype(bf16)
    up_out[...] = lax.dot_general(
        tokens_t[...], deltas[2], NT, preferred_element_type=f32
    ).astype(bf16)
    down_out[...] = jnp.dot(deltas[0], targets[...], preferred_element_type=f32).astype(bf16)


def shards(NZ, NY, NX, features, cotangent, gate_master, up_master, down_master):
    block, depth = features.shape
    hidden = gate_master.shape[1]
    tokens = block * NY * 2 * NX
    half = hidden // NZ // 2
    hops = NZ // 2
    span = tokens // 128
    vmem = pltpu.VMEM
    dma = pltpu.SemaphoreType.DMA
    plane = (2, NY, NX)
    scratch = [
        vmem(plane + (block, depth), bf16),
        vmem(plane + (block, depth), bf16),
        vmem((3, depth, hidden), f32),
        vmem((3, hidden, depth), bf16),
        vmem((depth, tokens), bf16),
        vmem((2, 3, NZ, 2 * half, tokens // 2), f32),
        vmem((2, hops, 2, 3, 2 * half, tokens // 2), bf16),
        vmem((2, hops, 2, 3, 2 * half, tokens // 2), bf16),
        vmem((NZ, block + 8, 128), f32),
        vmem((NZ, block + 8, 128), f32),
        vmem((NZ, block + 8, 128), f32),
        vmem((2,) + plane + (span + 1, block, 128), bf16),
        vmem((2, tokens, tokens), bf16),
        vmem((3, 2 * half, tokens), f32),
        vmem((3, 2 * half, tokens), f32),
        vmem((3, NZ, 2, half, tokens), bf16),
        vmem((3, 8, 128), f32),
        vmem((3, max(NZ, 2 * NY), 8, 128), f32),
        dma((5,)),
        dma((3, NZ, 2)),
        dma((4, 3, max(NX, NY))),
        dma((4, 3, max(NX, NY))),
        dma((2, NZ)),
        dma((2, NZ)),
        dma((2, hops, 2, 3)),
        dma((2, hops, 2, 3)),
        dma((2, hops, 3, 2)),
        dma((2, hops, 3, 2)),
        dma((3, max(NZ, 2 * NY))),
        dma((3, max(NZ, 2 * NY))),
    ]
    away = pl.BlockSpec(memory_space=pl.ANY)
    deltas, tokens_t, targets = pl.pallas_call(
        functools.partial(kernel, NZ, NY, NX),
        out_shape=(
            jax.ShapeDtypeStruct((3, NZ, 2, half, tokens), bf16),
            jax.ShapeDtypeStruct((depth, tokens), bf16),
            jax.ShapeDtypeStruct(plane + (block, depth), bf16),
        ),
        in_specs=[away] * 5,
        out_specs=(away, away, away),
        scratch_shapes=scratch,
        compiler_params=pltpu.CompilerParams(
            collective_id=0, has_side_effects=True, vmem_limit_bytes=56 * 1024 * 1024
        ),
        cost_estimate=pl.CostEstimate(
            flops=2 * 3 * hidden * depth * tokens,
            bytes_accessed=4 * 3 * hidden * depth,
            transcendentals=0,
        ),
    )(features, cotangent, gate_master, up_master, down_master)
    tile = hidden // 3
    return pl.pallas_call(
        gradients,
        grid=(hidden // tile,),
        out_shape=(
            jax.ShapeDtypeStruct((depth, hidden), bf16),
            jax.ShapeDtypeStruct((depth, hidden), bf16),
            jax.ShapeDtypeStruct((hidden, depth), bf16),
        ),
        in_specs=[
            pl.BlockSpec((depth, tokens), lambda i: (0, 0)),
            pl.BlockSpec((3, tile, tokens), lambda i: (0, i, 0)),
            pl.BlockSpec((tokens, depth), lambda i: (0, 0)),
        ],
        out_specs=(
            pl.BlockSpec((depth, tile), lambda i: (0, i)),
            pl.BlockSpec((depth, tile), lambda i: (0, i)),
            pl.BlockSpec((tile, depth), lambda i: (i, 0)),
        ),
        compiler_params=pltpu.CompilerParams(vmem_limit_bytes=60 * 1024 * 1024),
        cost_estimate=pl.CostEstimate(
            flops=2 * 3 * hidden * depth * tokens,
            bytes_accessed=2 * (5 * hidden * tokens + 3 * hidden * depth),
            transcendentals=0,
        ),
    )(tokens_t, deltas.reshape(3, hidden, tokens), targets.reshape(tokens, depth))


def solution(mesh):
    placed = (
        P(("col", "depth"), "row"),
        P(("col", "depth"), "row"),
        P("row", ("col", "depth")),
        P("row", ("col", "depth")),
        P(("col", "depth"), "row"),
    )
    return jax.shard_map(
        functools.partial(shards, mesh.shape["row"], mesh.shape["col"] // 2, mesh.shape["depth"]),
        mesh=mesh,
        in_specs=placed,
        out_specs=(
            P("row", ("col", "depth")),
            P("row", ("col", "depth")),
            P(("col", "depth"), "row"),
        ),
        check_vma=False,
    )
```

```python
import functools

import jax
import jax.numpy as jnp
from jax import lax
from jax.experimental import pallas as pl
from jax.experimental.pallas import tpu as pltpu
from jax.sharding import PartitionSpec as P

radius = 0.3
MESH = pl.DeviceIdType.MESH
NT = (((1,), (1,)), ((), ()))
f32, bf16 = jnp.float32, jnp.bfloat16


def pointwise(gate_sum, up_sum, back_sum):
    sigmoid_gate = jax.nn.sigmoid(gate_sum)
    swish_gate = gate_sum * sigmoid_gate
    activation = (swish_gate * up_sum).astype(bf16)
    gate_delta = (
        back_sum * up_sum * sigmoid_gate * (1.0 + gate_sum * (1.0 - sigmoid_gate))
    ).astype(bf16)
    up_delta = (back_sum * swish_gate).astype(bf16)
    return (activation, gate_delta, up_delta)


def fold(x):
    rows, lanes = x.shape
    x = jnp.sum(x.reshape(rows // 8, 8, lanes), axis=0)
    return sum(x[:, i : i + 128] for i in range(0, lanes, 128))


def all_gather_plane(NY, NX, y, x, at_x, at_y, sibling, remote, arrive, leave):
    every = slice(None)

    def parts(order):
        if order == "xy":
            return (
                NX, NY, at_x, at_y,
                lambda core: (core, y, every),
                lambda i: (0, y, (x - i + NX) % NX),
                lambda core, i: (core, (y - i + NY) % NY, every),
            )
        return (
            NY, NX, at_y, at_x,
            lambda core: (core, every, x),
            lambda i: (0, (y - i + NY) % NY, x),
            lambda core, i: (core, every, (x - i + NX) % NX),
        )

    own = (0, y, x)

    def start(flow):
        view, order, ss, rs = flow
        n1, n2, first, second, line, one, lines = parts(order)
        for i in range(1, n1):
            remote(view(own), view(own), ss.at[0, i], rs.at[0, i], first(i)).start()

    def middle(flow):
        view, order, ss, rs = flow
        n1, n2, first, second, line, one, lines = parts(order)
        for i in range(1, n1):
            arrive(view(one(i)), ss.at[0, i], rs.at[0, i])
        for i in range(1, n2):
            remote(view(line(0)), view(line(0)), ss.at[1, i], rs.at[1, i], second(i)).start()
        remote(view(line(0)), view(line(1)), ss.at[2, 0], rs.at[2, 0], sibling).start()

    def across(flow):
        view, order, ss, rs = flow
        n1, n2, first, second, line, one, lines = parts(order)
        for i in range(1, n2):
            arrive(view(lines(0, i)), ss.at[1, i], rs.at[1, i])
            remote(
                view(lines(0, i)), view(lines(1, i)), ss.at[2, i], rs.at[2, i], sibling
            ).start()

    def finish(flow):
        view, order, ss, rs = flow
        n1, n2, first, second, line, one, lines = parts(order)
        for i in range(1, n2):
            arrive(view(lines(1, i)), ss.at[2, i], rs.at[2, i])

    def sibling_line(flow):
        view, order, ss, rs = flow
        arrive(view(parts(order)[4](1)), ss.at[2, 0], rs.at[2, 0])

    def sent(flow):
        view, order, ss, rs = flow
        n1, n2, first, second, line, one, lines = parts(order)
        for i in range(1, n1):
            leave(view(own), ss.at[0, i], rs.at[0, i])
        for i in range(1, n2):
            leave(view(line(0)), ss.at[1, i], rs.at[1, i])
        for i in range(n2):
            leave(view(lines(0, i)), ss.at[2, i], rs.at[2, i])

    return start, middle, across, sibling_line, finish, sent


def peak_of(x):
    rows, lanes = x.shape
    x = jnp.max(jnp.abs(x).reshape(rows // 8, 8, lanes), axis=0)
    return functools.reduce(jnp.maximum, [x[:, i : i + 128] for i in range(0, lanes, 128)])


def powers(largest):
    scale = jnp.ones_like(largest)
    inverse = jnp.ones_like(largest)
    for e in (64, 32, 16, 8):
        over = largest >= 2.0**e
        under = largest < 2.0**-e
        down = jnp.where(over, 2.0**-e, jnp.where(under, 2.0**e, 1.0))
        up = jnp.where(over, 2.0**e, jnp.where(under, 2.0**-e, 1.0))
        largest, scale, inverse = largest * down, scale * down, inverse * up
    return scale, inverse


def kernel(
    NZ, NY, NX,
    features, cotangent, gate_master, up_master, down_master,
    deltas_out, tokens_t_out, targets_out,
    tok, tgt, stage, weights, tokens_t, part, outbox, inbox,
    kpart, kin, kown, heads, codes, kplane, gram, vectors, sums, steps, deltas, energy, energy_in,
    local_sem, out_sem, plane_s, plane_r, kz_s, kz_r, ch_s, ch_r, ag_s, ag_r, en_s, en_r,
):
    z, c, x = lax.axis_index("row"), lax.axis_index("col"), lax.axis_index("depth")
    y, k = c // 2, c % 2
    hidden = weights.shape[1]
    depth, tokens = tokens_t.shape
    own = hidden // NZ
    half = own // 2
    side = tokens // 2
    block = features.shape[0]
    span = tokens // 128

    def at_z(i):
        return ((z + i + NZ) % NZ, c, x)

    def at_y(i):
        return (z, ((y + i) % NY) * 2 + k, x)

    def at_x(i):
        return (z, c, (x + i) % NX)

    def at_pair(q):
        return (z, ((y + q // 2) % NY) * 2 + (k + q % 2) % 2, x)

    sibling = at_pair(1)

    def remote(src, dst, ssem, rsem, device):
        return pltpu.make_async_remote_copy(
            src_ref=src, dst_ref=dst, send_sem=ssem, recv_sem=rsem,
            device_id=device, device_id_type=MESH,
        )

    def arrive(dst, ssem, rsem):
        remote(dst, dst, ssem, rsem, sibling).wait_recv()

    def leave(src, ssem, rsem):
        remote(src, src, ssem, rsem, sibling).wait_send()

    masters = (gate_master, up_master, down_master)
    loads = [pltpu.make_async_copy(masters[m], stage.at[m], local_sem.at[m]) for m in range(3)]
    loads += [
        pltpu.make_async_copy(features, tok.at[0, y, x], local_sem.at[3]),
        pltpu.make_async_copy(cotangent, tgt.at[0, y, x], local_sem.at[4]),
    ]
    for load in loads[3:] + loads[:3]:
        load.start()

    barrier = pltpu.get_barrier_semaphore()
    partners = (
        [at_x(i) for i in range(1, NX)]
        + [at_pair(q) for q in range(1, 2 * NY)]
        + [at_z(i) for i in range(1, NZ)]
    )
    for device in partners:
        pl.semaphore_signal(barrier, inc=1, device_id=device, device_id_type=MESH)
    loads[3].wait()
    loads[4].wait()
    pl.semaphore_wait(barrier, len(partners))

    start, middle, across, sibling_line, finish, sent = all_gather_plane(
        NY, NX, y, x, at_x, at_y, sibling, remote, arrive, leave
    )

    flows_in = (
        (lambda where: tok.at[where], "xy", plane_s.at[0], plane_r.at[0]),
        (lambda where: tgt.at[where], "yx", plane_s.at[1], plane_r.at[1]),
    )
    flows_gram = tuple(
        (lambda where, g=g: kplane.at[(g, *where)], order, plane_s.at[2 + g], plane_r.at[2 + g])
        for g, order in enumerate(("xy", "yx"))
    )

    def run(step, flows):
        for flow in flows:
            step(flow)

    def prepare(m, transpose):
        loads[m].wait()
        rows = 128

        def body(i, total):
            r = pl.ds(pl.multiple_of(i * rows, rows), rows)
            piece = stage[m, r, :]
            if transpose:
                weights[m, :, r] = piece.astype(bf16).T
            else:
                weights[m, r, :] = piece.astype(bf16)
            energy_now, peak = total
            return energy_now + fold(piece * piece), jnp.maximum(peak, peak_of(piece))

        zero = jnp.zeros((8, 128), f32)
        return lax.fori_loop(0, hidden // rows, body, (zero, zero))

    def hops(d, h):
        return NZ // 2 if d == h else NZ // 2 - 1

    signs = (1, -1)

    def encode(total, m):
        total = total * codes[m : m + 1, 0:1]
        return (total * jnp.abs(total)).astype(bf16)

    def decode(square, m):
        square = square.astype(f32)
        root = square * lax.rsqrt(jnp.maximum(jnp.abs(square), 1e-37))
        return root * codes[4 + m : 5 + m, 0:1]

    def received(d, t, h, m):
        arrive(inbox.at[d, t, h, m], ch_s.at[d, t, h, m], ch_r.at[d, t, h, m])
        return decode(inbox[d, t, h, m], m) if t >= 2 else inbox[d, t, h, m].astype(f32)

    def chain_send(t, h, m):
        for d, sign in enumerate(signs):
            n = hops(d, h)
            if t >= n:
                continue
            owner = (z + sign * (n - t) + NZ) % NZ
            total = part[h, m, owner]
            if t > 0:
                total = total + received(d, t - 1, h, m)
            outbox[d, t, h, m] = encode(total, m) if t >= 2 else total.astype(bf16)
            remote(
                outbox.at[d, t, h, m], inbox.at[d, t, h, m],
                ch_s.at[d, t, h, m], ch_r.at[d, t, h, m], at_z(sign),
            ).start()

    def multiply(h, m):
        every = tok if m < 2 else tgt
        wide = hidden // 2
        for i in range(2):
            part[h, m, i * (NZ // 2) : (i + 1) * (NZ // 2)] = lax.dot_general(
                weights[m, i * wide : (i + 1) * wide, :],
                every[h].reshape(side, depth), NT, preferred_element_type=f32,
            ).reshape(NZ // 2, own, side)

    def loop3(f):
        def body(m, carry):
            f(m)
            return carry

        lax.fori_loop(0, 3, body, 0)

    def gram_partial():
        first_lanes = lax.broadcasted_iota(jnp.int32, (1, 128), 1) < 64
        head, scales = [], []
        for peak in (peak_of(tok[0].reshape(side, depth).astype(f32)),
                     peak_of(tgt[0].reshape(side, depth).astype(f32)), *weight_peaks):
            peak = jnp.max(jnp.max(peak, axis=0, keepdims=True), axis=1, keepdims=True)
            scale, inverse = powers(peak)
            scales.append(scale)
            head.append(jnp.where(first_lanes, inverse, scale))
        head = jnp.concatenate(head + [jnp.ones((3, 128), f32)], axis=0)
        for g, every in enumerate((tok, tgt)):
            pair = jnp.concatenate(
                [(every[0, y, x].astype(f32) * scales[g]).astype(bf16), every[1, y, x]], axis=0
            )
            rows = lax.dot_general(
                pair, every[0].reshape(side, depth), NT, preferred_element_type=f32
            ) * scales[g]
            for p in range(span):
                r, j = p // (span // 2) * block, p % (span // 2) * 128
                kpart[g * span + p, 0:block] = rows[r : r + block, j : j + 128]
                kpart[g * span + p, block : block + 8] = head
        for i in range(1, NZ):
            remote(
                kpart.at[(z + i) % NZ], kin.at[i], kz_s.at[0, i], kz_r.at[0, i], at_z(i)
            ).start()

    def gram_reduce():
        kin[0] = kpart[z]
        for i in range(1, NZ):
            arrive(kin.at[i], kz_s.at[0, i], kz_r.at[0, i])
        inverses = functools.reduce(jnp.maximum, [kin[i, block : block + 8] for i in range(NZ)])
        scales = functools.reduce(jnp.minimum, [kin[i, block : block + 8] for i in range(NZ)])
        heads[0], heads[1] = inverses, scales
        for m in range(3):
            g, w = m // 2, 2 + m
            code = scales[g : g + 1, 64:65] * scales[w : w + 1, 64:65]
            back = inverses[g : g + 1, 0:1] * inverses[w : w + 1, 0:1]
            code = jnp.clip(code, 2.0**-100, 2.0**90) * 2.0**30
            back = jnp.clip(back, 2.0**-90, 2.0**100) * 2.0**-30
            codes[m : m + 1] = jnp.broadcast_to(code, (1, 128))
            codes[4 + m : 5 + m] = jnp.broadcast_to(back, (1, 128))
        is_tok = z < span
        scale = jnp.where(is_tok, scales[0:1, 64:65], scales[1:2, 64:65])
        squared = z % span < span // 2
        total = jnp.zeros((block, 128), f32)
        for i in range(NZ):
            ratio = scale * jnp.where(
                is_tok, kin[i, block : block + 1, 0:1], kin[i, block + 1 : block + 2, 0:1]
            )
            total = total + kin[i, 0:block] * ratio * jnp.where(squared, ratio, 1.0)
        kown[z] = total
        for i in range(1, NZ):
            remote(kown.at[z], kown.at[z], kz_s.at[1, i], kz_r.at[1, i], at_z(i)).start()

    def gram_rows():
        for i in range(1, NZ):
            arrive(kown.at[(z - i + NZ) % NZ], kz_s.at[1, i], kz_r.at[1, i])
        first = (y * NX + x) * block
        rows = lax.broadcasted_iota(jnp.int32, (block, 128), 0)
        columns = lax.broadcasted_iota(jnp.int32, (block, 128), 1)
        for g in range(2):
            rest = []
            for p in range(span):
                piece = kown[g * span + p]
                high = piece.astype(bf16)
                kplane[g, 0, y, x, p] = high
                if p < span // 2:
                    low = jnp.where(
                        columns + p * 128 == rows + first, piece - high.astype(f32), 0.0
                    )
                    rest.append(jnp.sum(low, axis=0, keepdims=True))
            rest.append(jnp.broadcast_to(heads[0, g : g + 1, 0:1], (1, 128)))
            rest.append(jnp.zeros((block - span // 2 - 1, 128), f32))
            kplane[g, 0, y, x, span] = jnp.concatenate(rest, axis=0).astype(bf16)

    run(start, flows_in)
    weight_energy, gate_peak = prepare(0, True)
    run(middle, flows_in)
    more, up_peak = prepare(1, True)
    last, down_peak = prepare(2, False)
    weight_energy = weight_energy + more + last
    weight_peaks = (gate_peak, up_peak, down_peak)
    copies = []

    def transposed():
        tokens_t[...] = tok[...].reshape(tokens, depth).T
        copies.append(pltpu.make_async_copy(tokens_t, tokens_t_out, local_sem.at[0]))
        copies.append(pltpu.make_async_copy(tgt, targets_out, local_sem.at[1]))
        for copy in copies:
            copy.start()

    def gram_whole():
        for g in range(2):
            low, back = [], []
            for core in range(2):
                for p in range(span):
                    first = (core + p // (span // 2)) % 2 * side
                    j = core * side + p % (span // 2) * 128
                    gram[g, first : first + side, j : j + 128] = kplane[
                        g, core, :, :, p
                    ].reshape(side, 128)
                lows = kplane[g, core, :, :, span].reshape(side // block, block, 128).astype(f32)
                back.append(lows[0, span // 2 : span // 2 + 1])
                lows = jnp.sum(lows, axis=0)
                low += [lows[j : j + 1] for j in range(span // 2)]
            vectors[g, 0:1] = jnp.concatenate(low, axis=1)
            vectors[2 + g, 0:1] = jnp.concatenate(
                [b for b in back for _ in range(span // 2)], axis=1
            )

    def spread(t, m):
        for h in range(2):
            for d, sign in enumerate(signs):
                n = hops(d, h)
                owner = (z - sign * t + NZ) % NZ
                there = sums.at[m, owner, h]
                if 0 < t <= n:
                    arrive(there, ag_s.at[d, t - 1, m, h], ag_r.at[d, t - 1, m, h])
                if t < n:
                    remote(
                        there, there, ag_s.at[d, t, m, h], ag_r.at[d, t, m, h], at_z(sign)
                    ).start()

    def chain_last(m):
        halves = []
        for h in range(2):
            total = part[h, m, z]
            for d in range(2):
                total = total + received(d, hops(d, h) - 1, h, m)
            halves.append(total)
        total = jnp.concatenate(halves, axis=1)
        sums[m, z] = encode(total, m).reshape(2, half, tokens)
        spread(0, m)

    def sums_of(owner):
        return [decode(sums[m, owner].reshape(own, tokens), m) for m in range(3)]

    def gram_dot(delta, g):
        own_half = lax.broadcasted_iota(jnp.int32, (1, tokens), 1) < side
        plain = delta.astype(f32)
        scaled = plain * vectors[2 + g, 0:1]
        halves = []
        for core in range(2):
            mixed = jnp.where(own_half == (core == 0), scaled, plain).astype(bf16)
            halves.append(
                jnp.dot(
                    mixed, gram[g, :, core * side : (core + 1) * side], preferred_element_type=f32
                )
            )
        return scaled, jnp.concatenate(halves, axis=1) + scaled * vectors[g, 0:1]

    def first_pass(owner, own_units=False):
        activation, gate_delta, up_delta = pointwise(*sums_of(owner))
        scaled, both = gram_dot(jnp.concatenate([gate_delta, up_delta], axis=0), 0)
        back_scaled, back = gram_dot(activation, 1)
        steps[0, owner], steps[1, owner], steps[2, owner] = both[:own], both[own:], back
        if own_units:
            return fold(scaled * both) + fold(back_scaled * back)

    def to_hbm(m, owner):
        return pltpu.make_async_copy(deltas.at[m, owner], deltas_out.at[m, owner], out_sem.at[m, owner])

    def second_pass(owner):
        parts = [
            total + vectors[4 if m < 2 else 5, 0:1] * steps[m, owner]
            for m, total in enumerate(sums_of(owner))
        ]
        for m, part_m in enumerate(pointwise(*parts)):
            deltas[m, owner] = part_m
            to_hbm(m, owner).start()

    def at_distance(f, t):
        if t == 0 or 2 * t == NZ:
            f((z + t) % NZ)
            return

        def body(i, carry):
            f((z + (1 - 2 * i) * t + NZ) % NZ)
            return carry

        lax.fori_loop(0, 2, body, 0)

    spans = ((NX, at_x), (2 * NY, at_pair), (NZ, at_z))

    def energy_send(i, tile):
        energy[i] = tile
        count, where = spans[i]
        for q in range(1, count):
            remote(
                energy.at[i], energy_in.at[i, q], en_s.at[i, q], en_r.at[i, q], where(q)
            ).start()

    def energy_own():
        gradient_energy = first_pass(z, own_units=True)
        energy_send(
            0,
            jnp.concatenate(
                [
                    jnp.sum(weight_energy, axis=0, keepdims=True),
                    jnp.sum(gradient_energy, axis=0, keepdims=True),
                    jnp.zeros((6, 128), f32),
                ],
                axis=0,
            ),
        )

    def energy_wait(i):
        tile = energy[i]
        for q in range(1, spans[i][0]):
            arrive(energy_in.at[i, q], en_s.at[i, q], en_r.at[i, q])
            tile = tile + energy_in[i, q]
        if i + 1 < len(spans):
            energy_send(i + 1, tile)
            return
        totals = jnp.sum(tile, axis=1, keepdims=True)
        step_scale = (
            radius * jnp.sqrt(totals[0:1]) / jnp.sqrt(jnp.maximum(totals[1:2], 0.0) + 1e-06)
        )
        for g in range(2):
            vectors[4 + g, 0:1] = step_scale * vectors[2 + g, 0:1]

    def early_sent():
        for flow in flows_in + flows_gram:
            sent(flow)
        for i in range(1, NZ):
            leave(kpart.at[(z + i) % NZ], kz_s.at[0, i], kz_r.at[0, i])
            leave(kown.at[z], kz_s.at[1, i], kz_r.at[1, i])

        def chains_sent(m):
            for d in range(2):
                for h in range(2):
                    for t in range(hops(d, h)):
                        leave(outbox.at[d, t, h, m], ch_s.at[d, t, h, m], ch_r.at[d, t, h, m])

        loop3(chains_sent)
        for copy in copies:
            copy.wait()

    across(flows_in[0])
    multiply(0, 0)
    chain_send(0, 0, 0)
    multiply(0, 1)
    chain_send(0, 0, 1)
    across(flows_in[1])
    run(sibling_line, flows_in)
    gram_partial()
    multiply(0, 2)
    chain_send(0, 0, 2)
    run(finish, flows_in)
    for m in range(3):
        multiply(1, m)
        chain_send(0, 1, m)
    for m in range(3):
        chain_send(1, 0, m)
    gram_reduce()
    for m in range(3):
        chain_send(1, 1, m)
    for m in range(3):
        chain_send(2, 0, m)
    gram_rows()
    run(start, flows_gram)
    transposed()
    for m in range(3):
        chain_send(2, 1, m)
    for m in range(3):
        chain_send(3, 0, m)
    middle(flows_gram[0])
    middle(flows_gram[1])
    for m in range(3):
        chain_send(3, 1, m)
    for m in range(3):
        chain_last(m)
    across(flows_gram[0])
    across(flows_gram[1])
    sibling_line(flows_gram[0])
    finish(flows_gram[0])
    sibling_line(flows_gram[1])
    finish(flows_gram[1])
    gram_whole()
    energy_own()
    loop3(functools.partial(spread, 1))
    energy_wait(0)
    at_distance(first_pass, 1)
    energy_wait(1)
    loop3(functools.partial(spread, 2))
    early_sent()
    energy_wait(2)
    at_distance(second_pass, 0)
    at_distance(second_pass, 1)
    at_distance(first_pass, 2)
    at_distance(second_pass, 2)
    loop3(functools.partial(spread, 3))
    at_distance(first_pass, 3)
    at_distance(second_pass, 3)
    loop3(functools.partial(spread, 4))
    at_distance(first_pass, 4)
    at_distance(second_pass, 4)

    for i, (count, where) in enumerate(spans):
        for q in range(1, count):
            leave(energy.at[i], en_s.at[i, q], en_r.at[i, q])

    def late_sent(m):
        for d, sign in enumerate(signs):
            for h in range(2):
                for t in range(hops(d, h)):
                    leave(
                        sums.at[m, (z - sign * t + NZ) % NZ, h],
                        ag_s.at[d, t, m, h], ag_r.at[d, t, m, h],
                    )
        for owner in range(NZ):
            to_hbm(m, owner).wait()

    loop3(late_sent)


def gradients(tokens_t, deltas, targets, gate_out, up_out, down_out):
    gate_out[...] = lax.dot_general(
        tokens_t[...], deltas[1], NT, preferred_element_type=f32
    ).astype(bf16)
    up_out[...] = lax.dot_general(
        tokens_t[...], deltas[2], NT, preferred_element_type=f32
    ).astype(bf16)
    down_out[...] = jnp.dot(deltas[0], targets[...], preferred_element_type=f32).astype(bf16)


def shards(NZ, NY, NX, features, cotangent, gate_master, up_master, down_master):
    block, depth = features.shape
    hidden = gate_master.shape[1]
    tokens = block * NY * 2 * NX
    half = hidden // NZ // 2
    hops = NZ // 2
    span = tokens // 128
    vmem = pltpu.VMEM
    dma = pltpu.SemaphoreType.DMA
    plane = (2, NY, NX)
    scratch = [
        vmem(plane + (block, depth), bf16),
        vmem(plane + (block, depth), bf16),
        vmem((3, depth, hidden), f32),
        vmem((3, hidden, depth), bf16),
        vmem((depth, tokens), bf16),
        vmem((2, 3, NZ, 2 * half, tokens // 2), f32),
        vmem((2, hops, 2, 3, 2 * half, tokens // 2), bf16),
        vmem((2, hops, 2, 3, 2 * half, tokens // 2), bf16),
        vmem((NZ, block + 8, 128), f32),
        vmem((NZ, block + 8, 128), f32),
        vmem((NZ, block, 128), f32),
        vmem((2, 8, 128), f32),
        vmem((8, 128), f32),
        vmem((2,) + plane + (span + 1, block, 128), bf16),
        vmem((2, tokens, tokens), bf16),
        vmem((6, 8, tokens), f32),
        vmem((3, NZ, 2, half, tokens), bf16),
        vmem((3, NZ, 2 * half, tokens), f32),
        vmem((3, NZ, 2 * half, tokens), bf16),
        vmem((3, 8, 128), f32),
        vmem((3, max(NZ, 2 * NY), 8, 128), f32),
        dma((5,)),
        dma((3, NZ)),
        dma((4, 3, max(NX, NY))),
        dma((4, 3, max(NX, NY))),
        dma((2, NZ)),
        dma((2, NZ)),
        dma((2, hops, 2, 3)),
        dma((2, hops, 2, 3)),
        dma((2, hops, 3, 2)),
        dma((2, hops, 3, 2)),
        dma((3, max(NZ, 2 * NY))),
        dma((3, max(NZ, 2 * NY))),
    ]
    away = pl.BlockSpec(memory_space=pl.ANY)
    deltas, tokens_t, targets = pl.pallas_call(
        functools.partial(kernel, NZ, NY, NX),
        out_shape=(
            jax.ShapeDtypeStruct((3, NZ, 2 * half, tokens), bf16),
            jax.ShapeDtypeStruct((depth, tokens), bf16),
            jax.ShapeDtypeStruct(plane + (block, depth), bf16),
        ),
        in_specs=[away] * 5,
        out_specs=(away, away, away),
        scratch_shapes=scratch,
        compiler_params=pltpu.CompilerParams(
            collective_id=0, has_side_effects=True, vmem_limit_bytes=56 * 1024 * 1024
        ),
        cost_estimate=pl.CostEstimate(
            flops=2 * 3 * hidden * depth * tokens,
            bytes_accessed=4 * 3 * hidden * depth,
            transcendentals=0,
        ),
    )(features, cotangent, gate_master, up_master, down_master)
    tile = hidden // 3
    return pl.pallas_call(
        gradients,
        grid=(hidden // tile,),
        out_shape=(
            jax.ShapeDtypeStruct((depth, hidden), bf16),
            jax.ShapeDtypeStruct((depth, hidden), bf16),
            jax.ShapeDtypeStruct((hidden, depth), bf16),
        ),
        in_specs=[
            pl.BlockSpec((depth, tokens), lambda i: (0, 0)),
            pl.BlockSpec((3, tile, tokens), lambda i: (0, i, 0)),
            pl.BlockSpec((tokens, depth), lambda i: (0, 0)),
        ],
        out_specs=(
            pl.BlockSpec((depth, tile), lambda i: (0, i)),
            pl.BlockSpec((depth, tile), lambda i: (0, i)),
            pl.BlockSpec((tile, depth), lambda i: (i, 0)),
        ),
        compiler_params=pltpu.CompilerParams(vmem_limit_bytes=60 * 1024 * 1024),
        cost_estimate=pl.CostEstimate(
            flops=2 * 3 * hidden * depth * tokens,
            bytes_accessed=2 * (5 * hidden * tokens + 3 * hidden * depth),
            transcendentals=0,
        ),
    )(tokens_t, deltas.reshape(3, hidden, tokens), targets.reshape(tokens, depth))


def solution(mesh):
    placed = (
        P(("col", "depth"), "row"),
        P(("col", "depth"), "row"),
        P("row", ("col", "depth")),
        P("row", ("col", "depth")),
        P(("col", "depth"), "row"),
    )
    return jax.shard_map(
        functools.partial(shards, mesh.shape["row"], mesh.shape["col"] // 2, mesh.shape["depth"]),
        mesh=mesh,
        in_specs=placed,
        out_specs=(
            P("row", ("col", "depth")),
            P("row", ("col", "depth")),
            P(("col", "depth"), "row"),
        ),
        check_vma=False,
    )
```

```python
import functools

import jax
import jax.numpy as jnp
from jax import lax
from jax.experimental import pallas as pl
from jax.experimental.pallas import tpu as pltpu
from jax.sharding import PartitionSpec as P

radius = 0.3
MESH = pl.DeviceIdType.MESH
NT = (((1,), (1,)), ((), ()))
f32, bf16 = jnp.float32, jnp.bfloat16


def pointwise(gate_sum, up_sum, back_sum):
    sigmoid_gate = jax.nn.sigmoid(gate_sum)
    swish_gate = gate_sum * sigmoid_gate
    activation = (swish_gate * up_sum).astype(bf16)
    gate_delta = (
        back_sum * up_sum * sigmoid_gate * (1.0 + gate_sum * (1.0 - sigmoid_gate))
    ).astype(bf16)
    up_delta = (back_sum * swish_gate).astype(bf16)
    return (activation, gate_delta, up_delta)


def fold(x):
    rows, lanes = x.shape
    x = jnp.sum(x.reshape(rows // 8, 8, lanes), axis=0)
    return sum(x[:, i : i + 128] for i in range(0, lanes, 128))


def all_gather_plane(NY, NX, y, x, at_x, at_y, sibling, remote, arrive, leave):
    every = slice(None)

    def parts(order):
        if order == "xy":
            return (
                NX, NY, at_x, at_y,
                lambda core: (core, y, every),
                lambda i: (0, y, (x - i + NX) % NX),
                lambda core, i: (core, (y - i + NY) % NY, every),
            )
        return (
            NY, NX, at_y, at_x,
            lambda core: (core, every, x),
            lambda i: (0, (y - i + NY) % NY, x),
            lambda core, i: (core, every, (x - i + NX) % NX),
        )

    own = (0, y, x)

    def start(flow):
        view, order, ss, rs = flow
        n1, n2, first, second, line, one, lines = parts(order)
        for i in range(1, n1):
            remote(view(own), view(own), ss.at[0, i], rs.at[0, i], first(i)).start()

    def middle(flow):
        view, order, ss, rs = flow
        n1, n2, first, second, line, one, lines = parts(order)
        for i in range(1, n1):
            arrive(view(one(i)), ss.at[0, i], rs.at[0, i])
        for i in range(1, n2):
            remote(view(line(0)), view(line(0)), ss.at[1, i], rs.at[1, i], second(i)).start()
        remote(view(line(0)), view(line(1)), ss.at[2, 0], rs.at[2, 0], sibling).start()

    def across(flow):
        view, order, ss, rs = flow
        n1, n2, first, second, line, one, lines = parts(order)
        for i in range(1, n2):
            arrive(view(lines(0, i)), ss.at[1, i], rs.at[1, i])
            remote(
                view(lines(0, i)), view(lines(1, i)), ss.at[2, i], rs.at[2, i], sibling
            ).start()

    def finish(flow):
        view, order, ss, rs = flow
        n1, n2, first, second, line, one, lines = parts(order)
        for i in range(1, n2):
            arrive(view(lines(1, i)), ss.at[2, i], rs.at[2, i])

    def sibling_line(flow):
        view, order, ss, rs = flow
        arrive(view(parts(order)[4](1)), ss.at[2, 0], rs.at[2, 0])

    def sent(flow):
        view, order, ss, rs = flow
        n1, n2, first, second, line, one, lines = parts(order)
        for i in range(1, n1):
            leave(view(own), ss.at[0, i], rs.at[0, i])
        for i in range(1, n2):
            leave(view(line(0)), ss.at[1, i], rs.at[1, i])
        for i in range(n2):
            leave(view(lines(0, i)), ss.at[2, i], rs.at[2, i])

    return start, middle, across, sibling_line, finish, sent


def peak_of(x):
    rows, lanes = x.shape
    x = jnp.max(jnp.abs(x).reshape(rows // 8, 8, lanes), axis=0)
    return functools.reduce(jnp.maximum, [x[:, i : i + 128] for i in range(0, lanes, 128)])


def powers(largest):
    scale = jnp.ones_like(largest)
    inverse = jnp.ones_like(largest)
    for e in (64, 32, 16, 8):
        over = largest >= 2.0**e
        under = largest < 2.0**-e
        down = jnp.where(over, 2.0**-e, jnp.where(under, 2.0**e, 1.0))
        up = jnp.where(over, 2.0**e, jnp.where(under, 2.0**-e, 1.0))
        largest, scale, inverse = largest * down, scale * down, inverse * up
    return scale, inverse


def kernel(
    NZ, NY, NX,
    features, cotangent, gate_master, up_master, down_master,
    deltas_out, tokens_t_out, targets_out,
    tok, tgt, stage, weights, tokens_t, part, outbox, inbox,
    kpart, kin, kown, heads, codes, kplane, gram, vectors, sums, steps, deltas, energy, energy_in,
    local_sem, out_sem, plane_s, plane_r, kz_s, kz_r, ch_s, ch_r, ag_s, ag_r, en_s, en_r,
):
    z, c, x = lax.axis_index("row"), lax.axis_index("col"), lax.axis_index("depth")
    y, k = c // 2, c % 2
    hidden = weights.shape[1]
    depth, tokens = tokens_t.shape
    own = hidden // NZ
    half = own // 2
    side = tokens // 2
    block = features.shape[0]
    span = tokens // 128

    def at_z(i):
        return ((z + i + NZ) % NZ, c, x)

    def at_y(i):
        return (z, ((y + i) % NY) * 2 + k, x)

    def at_x(i):
        return (z, c, (x + i) % NX)

    def at_pair(q):
        return (z, ((y + q // 2) % NY) * 2 + (k + q % 2) % 2, x)

    sibling = at_pair(1)

    def remote(src, dst, ssem, rsem, device):
        return pltpu.make_async_remote_copy(
            src_ref=src, dst_ref=dst, send_sem=ssem, recv_sem=rsem,
            device_id=device, device_id_type=MESH,
        )

    def arrive(dst, ssem, rsem):
        remote(dst, dst, ssem, rsem, sibling).wait_recv()

    def leave(src, ssem, rsem):
        remote(src, src, ssem, rsem, sibling).wait_send()

    masters = (gate_master, up_master, down_master)
    loads = [pltpu.make_async_copy(masters[m], stage.at[m], local_sem.at[m]) for m in range(3)]
    loads += [
        pltpu.make_async_copy(features, tok.at[0, y, x], local_sem.at[3]),
        pltpu.make_async_copy(cotangent, tgt.at[0, y, x], local_sem.at[4]),
    ]
    for load in loads[3:] + loads[:3]:
        load.start()

    barrier = pltpu.get_barrier_semaphore()
    partners = (
        [at_x(i) for i in range(1, NX)]
        + [at_pair(q) for q in range(1, 2 * NY)]
        + [at_z(i) for i in range(1, NZ)]
    )
    for device in partners:
        pl.semaphore_signal(barrier, inc=1, device_id=device, device_id_type=MESH)
    loads[3].wait()
    loads[4].wait()
    pl.semaphore_wait(barrier, len(partners))

    start, middle, across, sibling_line, finish, sent = all_gather_plane(
        NY, NX, y, x, at_x, at_y, sibling, remote, arrive, leave
    )

    flows_in = (
        (lambda where: tok.at[where], "xy", plane_s.at[0], plane_r.at[0]),
        (lambda where: tgt.at[where], "yx", plane_s.at[1], plane_r.at[1]),
    )
    flows_gram = tuple(
        (lambda where, g=g: kplane.at[(g, *where)], order, plane_s.at[2 + g], plane_r.at[2 + g])
        for g, order in enumerate(("xy", "yx"))
    )

    def run(step, flows):
        for flow in flows:
            step(flow)

    def prepare(m, transpose):
        loads[m].wait()
        rows = 128

        def body(i, total):
            r = pl.ds(pl.multiple_of(i * rows, rows), rows)
            piece = stage[m, r, :]
            if transpose:
                weights[m, :, r] = piece.astype(bf16).T
            else:
                weights[m, r, :] = piece.astype(bf16)
            energy_now, peak = total
            return energy_now + fold(piece * piece), jnp.maximum(peak, peak_of(piece))

        zero = jnp.zeros((8, 128), f32)
        return lax.fori_loop(0, hidden // rows, body, (zero, zero))

    def hops(d, h):
        return NZ // 2 if d == h else NZ // 2 - 1

    signs = (1, -1)

    def encode(total, m):
        total = total * codes[m : m + 1, 0:1]
        return (total * jnp.abs(total)).astype(bf16)

    def decode(square, m):
        square = square.astype(f32)
        root = square * lax.rsqrt(jnp.maximum(jnp.abs(square), 1e-37))
        return root * codes[4 + m : 5 + m, 0:1]

    def received(d, t, h, m):
        arrive(inbox.at[d, t, h, m], ch_s.at[d, t, h, m], ch_r.at[d, t, h, m])
        return decode(inbox[d, t, h, m], m) if t >= 2 else inbox[d, t, h, m].astype(f32)

    def chain_send(t, h, m):
        for d, sign in enumerate(signs):
            n = hops(d, h)
            if t >= n:
                continue
            owner = (z + sign * (n - t) + NZ) % NZ
            total = part[h, m, owner]
            if t > 0:
                total = total + received(d, t - 1, h, m)
            outbox[d, t, h, m] = encode(total, m) if t >= 2 else total.astype(bf16)
            remote(
                outbox.at[d, t, h, m], inbox.at[d, t, h, m],
                ch_s.at[d, t, h, m], ch_r.at[d, t, h, m], at_z(sign),
            ).start()

    def multiply(h, m):
        every = tok if m < 2 else tgt
        wide = hidden // 2
        for i in range(2):
            part[h, m, i * (NZ // 2) : (i + 1) * (NZ // 2)] = lax.dot_general(
                weights[m, i * wide : (i + 1) * wide, :],
                every[h].reshape(side, depth), NT, preferred_element_type=f32,
            ).reshape(NZ // 2, own, side)

    def loop3(f):
        def body(m, carry):
            f(m)
            return carry

        lax.fori_loop(0, 3, body, 0)

    def gram_partial():
        first_lanes = lax.broadcasted_iota(jnp.int32, (1, 128), 1) < 64
        head, scales = [], []
        for peak in (peak_of(tok[0].reshape(side, depth).astype(f32)),
                     peak_of(tgt[0].reshape(side, depth).astype(f32)), *weight_peaks):
            peak = jnp.max(jnp.max(peak, axis=0, keepdims=True), axis=1, keepdims=True)
            scale, inverse = powers(peak)
            scales.append(scale)
            head.append(jnp.where(first_lanes, inverse, scale))
        head = jnp.concatenate(head + [jnp.ones((3, 128), f32)], axis=0)
        for g, every in enumerate((tok, tgt)):
            pair = jnp.concatenate(
                [(every[0, y, x].astype(f32) * scales[g]).astype(bf16), every[1, y, x]], axis=0
            )
            rows = lax.dot_general(
                pair, every[0].reshape(side, depth), NT, preferred_element_type=f32
            ) * scales[g]
            for p in range(span):
                r, j = p // (span // 2) * block, p % (span // 2) * 128
                kpart[g * span + p, 0:block] = rows[r : r + block, j : j + 128]
                kpart[g * span + p, block : block + 8] = head
        for i in range(1, NZ):
            remote(
                kpart.at[(z + i) % NZ], kin.at[i], kz_s.at[0, i], kz_r.at[0, i], at_z(i)
            ).start()

    def gram_reduce():
        kin[0] = kpart[z]
        for i in range(1, NZ):
            arrive(kin.at[i], kz_s.at[0, i], kz_r.at[0, i])
        inverses = functools.reduce(jnp.maximum, [kin[i, block : block + 8] for i in range(NZ)])
        scales = functools.reduce(jnp.minimum, [kin[i, block : block + 8] for i in range(NZ)])
        heads[0], heads[1] = inverses, scales
        for m in range(3):
            g, w = m // 2, 2 + m
            code = scales[g : g + 1, 64:65] * scales[w : w + 1, 64:65]
            back = inverses[g : g + 1, 0:1] * inverses[w : w + 1, 0:1]
            code = jnp.clip(code, 2.0**-100, 2.0**90) * 2.0**30
            back = jnp.clip(back, 2.0**-90, 2.0**100) * 2.0**-30
            codes[m : m + 1] = jnp.broadcast_to(code, (1, 128))
            codes[4 + m : 5 + m] = jnp.broadcast_to(back, (1, 128))
        is_tok = z < span
        scale = jnp.where(is_tok, scales[0:1, 64:65], scales[1:2, 64:65])
        squared = z % span < span // 2
        total = jnp.zeros((block, 128), f32)
        for i in range(NZ):
            ratio = scale * jnp.where(
                is_tok, kin[i, block : block + 1, 0:1], kin[i, block + 1 : block + 2, 0:1]
            )
            total = total + kin[i, 0:block] * ratio * jnp.where(squared, ratio, 1.0)
        kown[z] = total
        for i in range(1, NZ):
            remote(kown.at[z], kown.at[z], kz_s.at[1, i], kz_r.at[1, i], at_z(i)).start()

    def gram_rows():
        for i in range(1, NZ):
            arrive(kown.at[(z - i + NZ) % NZ], kz_s.at[1, i], kz_r.at[1, i])
        first = (y * NX + x) * block
        rows = lax.broadcasted_iota(jnp.int32, (block, 128), 0)
        columns = lax.broadcasted_iota(jnp.int32, (block, 128), 1)
        for g in range(2):
            rest = []
            for p in range(span):
                piece = kown[g * span + p]
                high = piece.astype(bf16)
                kplane[g, 0, y, x, p] = high
                if p < span // 2:
                    low = jnp.where(
                        columns + p * 128 == rows + first, piece - high.astype(f32), 0.0
                    )
                    rest.append(jnp.sum(low, axis=0, keepdims=True))
            rest.append(jnp.broadcast_to(heads[0, g : g + 1, 0:1], (1, 128)))
            rest.append(jnp.zeros((block - span // 2 - 1, 128), f32))
            kplane[g, 0, y, x, span] = jnp.concatenate(rest, axis=0).astype(bf16)

    run(start, flows_in)
    weight_energy, gate_peak = prepare(0, True)
    run(middle, flows_in)
    more, up_peak = prepare(1, True)
    last, down_peak = prepare(2, False)
    weight_energy = weight_energy + more + last
    weight_peaks = (gate_peak, up_peak, down_peak)
    copies = []

    def transposed():
        tokens_t[...] = tok[...].reshape(tokens, depth).T
        copies.append(pltpu.make_async_copy(tokens_t, tokens_t_out, local_sem.at[0]))
        copies.append(pltpu.make_async_copy(tgt, targets_out, local_sem.at[1]))
        for copy in copies:
            copy.start()

    def gram_whole():
        for g in range(2):
            low, back = [], []
            for core in range(2):
                for p in range(span):
                    first = (core + p // (span // 2)) % 2 * side
                    j = core * side + p % (span // 2) * 128
                    gram[g, first : first + side, j : j + 128] = kplane[
                        g, core, :, :, p
                    ].reshape(side, 128)
                lows = kplane[g, core, :, :, span].reshape(side // block, block, 128).astype(f32)
                back.append(lows[0, span // 2 : span // 2 + 1])
                lows = jnp.sum(lows, axis=0)
                low += [lows[j : j + 1] for j in range(span // 2)]
            vectors[g, 0:1] = jnp.concatenate(low, axis=1)
            vectors[2 + g, 0:1] = jnp.concatenate(
                [b for b in back for _ in range(span // 2)], axis=1
            )

    def spread(t, m):
        for h in range(2):
            for d, sign in enumerate(signs):
                n = hops(d, h)
                owner = (z - sign * t + NZ) % NZ
                there = sums.at[m, owner, h]
                if 0 < t <= n:
                    arrive(there, ag_s.at[d, t - 1, m, h], ag_r.at[d, t - 1, m, h])
                if t < n:
                    remote(
                        there, there, ag_s.at[d, t, m, h], ag_r.at[d, t, m, h], at_z(sign)
                    ).start()

    def chain_last(m):
        halves = []
        for h in range(2):
            total = part[h, m, z]
            for d in range(2):
                total = total + received(d, hops(d, h) - 1, h, m)
            halves.append(total)
        total = jnp.concatenate(halves, axis=1)
        sums[m, z] = encode(total, m).reshape(2, half, tokens)
        spread(0, m)

    def sums_of(owner):
        return [decode(sums[m, owner].reshape(own, tokens), m) for m in range(3)]

    def gram_dot(delta, g):
        own_half = lax.broadcasted_iota(jnp.int32, (1, tokens), 1) < side
        plain = delta.astype(f32)
        scaled = plain * vectors[2 + g, 0:1]
        halves = []
        for core in range(2):
            mixed = jnp.where(own_half == (core == 0), scaled, plain).astype(bf16)
            halves.append(
                jnp.dot(
                    mixed, gram[g, :, core * side : (core + 1) * side], preferred_element_type=f32
                )
            )
        return scaled, jnp.concatenate(halves, axis=1) + scaled * vectors[g, 0:1]

    def first_pass(owner, own_units=False):
        activation, gate_delta, up_delta = pointwise(*sums_of(owner))
        scaled, both = gram_dot(jnp.concatenate([gate_delta, up_delta], axis=0), 0)
        back_scaled, back = gram_dot(activation, 1)
        steps[0, owner], steps[1, owner], steps[2, owner] = both[:own], both[own:], back
        if own_units:
            return fold(scaled * both) + fold(back_scaled * back)

    def to_hbm(m, owner):
        return pltpu.make_async_copy(deltas.at[m, owner], deltas_out.at[m, owner], out_sem.at[m, owner])

    def second_pass(owner):
        parts = [
            total + vectors[4 if m < 2 else 5, 0:1] * steps[m, owner]
            for m, total in enumerate(sums_of(owner))
        ]
        for m, part_m in enumerate(pointwise(*parts)):
            deltas[m, owner] = part_m
            to_hbm(m, owner).start()

    def at_distance(f, t):
        if t == 0 or 2 * t == NZ:
            f((z + t) % NZ)
            return

        def body(i, carry):
            f((z + (1 - 2 * i) * t + NZ) % NZ)
            return carry

        lax.fori_loop(0, 2, body, 0)

    spans = ((NX, at_x), (2 * NY, at_pair), (NZ, at_z))

    def energy_send(i, tile):
        energy[i] = tile
        count, where = spans[i]
        for q in range(1, count):
            remote(
                energy.at[i], energy_in.at[i, q], en_s.at[i, q], en_r.at[i, q], where(q)
            ).start()

    def energy_own():
        gradient_energy = first_pass(z, own_units=True)
        energy_send(
            0,
            jnp.concatenate(
                [
                    jnp.sum(weight_energy, axis=0, keepdims=True),
                    jnp.sum(gradient_energy, axis=0, keepdims=True),
                    jnp.zeros((6, 128), f32),
                ],
                axis=0,
            ),
        )

    def energy_wait(i):
        tile = energy[i]
        for q in range(1, spans[i][0]):
            arrive(energy_in.at[i, q], en_s.at[i, q], en_r.at[i, q])
            tile = tile + energy_in[i, q]
        if i + 1 < len(spans):
            energy_send(i + 1, tile)
            return
        totals = jnp.sum(tile, axis=1, keepdims=True)
        step_scale = (
            radius * jnp.sqrt(totals[0:1]) / jnp.sqrt(jnp.maximum(totals[1:2], 0.0) + 1e-06)
        )
        for g in range(2):
            vectors[4 + g, 0:1] = step_scale * vectors[2 + g, 0:1]

    def early_sent():
        for flow in flows_in + flows_gram:
            sent(flow)
        for i in range(1, NZ):
            leave(kpart.at[(z + i) % NZ], kz_s.at[0, i], kz_r.at[0, i])
            leave(kown.at[z], kz_s.at[1, i], kz_r.at[1, i])

        def chains_sent(m):
            for d in range(2):
                for h in range(2):
                    for t in range(hops(d, h)):
                        leave(outbox.at[d, t, h, m], ch_s.at[d, t, h, m], ch_r.at[d, t, h, m])

        loop3(chains_sent)
        for copy in copies:
            copy.wait()

    across(flows_in[0])
    multiply(0, 0)
    chain_send(0, 0, 0)
    multiply(0, 1)
    chain_send(0, 0, 1)
    across(flows_in[1])
    run(sibling_line, flows_in)
    gram_partial()
    multiply(0, 2)
    chain_send(0, 0, 2)
    run(finish, flows_in)
    for m in range(3):
        multiply(1, m)
        chain_send(0, 1, m)
    for m in range(3):
        chain_send(1, 0, m)
    gram_reduce()
    for m in range(3):
        chain_send(1, 1, m)
    for m in range(3):
        chain_send(2, 0, m)
    gram_rows()
    run(start, flows_gram)
    transposed()
    for m in range(3):
        chain_send(2, 1, m)
    for m in range(3):
        chain_send(3, 0, m)
    middle(flows_gram[0])
    middle(flows_gram[1])
    for m in range(3):
        chain_send(3, 1, m)
    for m in range(3):
        chain_last(m)
    across(flows_gram[0])
    across(flows_gram[1])
    sibling_line(flows_gram[0])
    finish(flows_gram[0])
    sibling_line(flows_gram[1])
    finish(flows_gram[1])
    gram_whole()
    energy_own()
    spread(1, 0)
    energy_wait(0)
    spread(1, 1)
    spread(1, 2)
    energy_wait(1)
    at_distance(first_pass, 1)
    spread(2, 0)
    spread(2, 1)
    energy_wait(2)
    at_distance(second_pass, 0)
    spread(2, 2)
    at_distance(second_pass, 1)
    at_distance(first_pass, 2)
    at_distance(second_pass, 2)
    spread(3, 0)
    spread(3, 1)
    spread(3, 2)
    early_sent()
    at_distance(first_pass, 3)
    at_distance(second_pass, 3)
    spread(4, 0)
    spread(4, 1)
    spread(4, 2)
    at_distance(first_pass, 4)
    at_distance(second_pass, 4)

    for i, (count, where) in enumerate(spans):
        for q in range(1, count):
            leave(energy.at[i], en_s.at[i, q], en_r.at[i, q])

    def late_sent(m):
        for d, sign in enumerate(signs):
            for h in range(2):
                for t in range(hops(d, h)):
                    leave(
                        sums.at[m, (z - sign * t + NZ) % NZ, h],
                        ag_s.at[d, t, m, h], ag_r.at[d, t, m, h],
                    )
        for owner in range(NZ):
            to_hbm(m, owner).wait()

    loop3(late_sent)


def gradients(tokens_t, deltas, targets, gate_out, up_out, down_out):
    gate_out[...] = lax.dot_general(
        tokens_t[...], deltas[1], NT, preferred_element_type=f32
    ).astype(bf16)
    up_out[...] = lax.dot_general(
        tokens_t[...], deltas[2], NT, preferred_element_type=f32
    ).astype(bf16)
    down_out[...] = jnp.dot(deltas[0], targets[...], preferred_element_type=f32).astype(bf16)


def shards(NZ, NY, NX, features, cotangent, gate_master, up_master, down_master):
    block, depth = features.shape
    hidden = gate_master.shape[1]
    tokens = block * NY * 2 * NX
    half = hidden // NZ // 2
    hops = NZ // 2
    span = tokens // 128
    vmem = pltpu.VMEM
    dma = pltpu.SemaphoreType.DMA
    plane = (2, NY, NX)
    scratch = [
        vmem(plane + (block, depth), bf16),
        vmem(plane + (block, depth), bf16),
        vmem((3, depth, hidden), f32),
        vmem((3, hidden, depth), bf16),
        vmem((depth, tokens), bf16),
        vmem((2, 3, NZ, 2 * half, tokens // 2), f32),
        vmem((2, hops, 2, 3, 2 * half, tokens // 2), bf16),
        vmem((2, hops, 2, 3, 2 * half, tokens // 2), bf16),
        vmem((NZ, block + 8, 128), f32),
        vmem((NZ, block + 8, 128), f32),
        vmem((NZ, block, 128), f32),
        vmem((2, 8, 128), f32),
        vmem((8, 128), f32),
        vmem((2,) + plane + (span + 1, block, 128), bf16),
        vmem((2, tokens, tokens), bf16),
        vmem((6, 8, tokens), f32),
        vmem((3, NZ, 2, half, tokens), bf16),
        vmem((3, NZ, 2 * half, tokens), f32),
        vmem((3, NZ, 2 * half, tokens), bf16),
        vmem((3, 8, 128), f32),
        vmem((3, max(NZ, 2 * NY), 8, 128), f32),
        dma((5,)),
        dma((3, NZ)),
        dma((4, 3, max(NX, NY))),
        dma((4, 3, max(NX, NY))),
        dma((2, NZ)),
        dma((2, NZ)),
        dma((2, hops, 2, 3)),
        dma((2, hops, 2, 3)),
        dma((2, hops, 3, 2)),
        dma((2, hops, 3, 2)),
        dma((3, max(NZ, 2 * NY))),
        dma((3, max(NZ, 2 * NY))),
    ]
    away = pl.BlockSpec(memory_space=pl.ANY)
    deltas, tokens_t, targets = pl.pallas_call(
        functools.partial(kernel, NZ, NY, NX),
        out_shape=(
            jax.ShapeDtypeStruct((3, NZ, 2 * half, tokens), bf16),
            jax.ShapeDtypeStruct((depth, tokens), bf16),
            jax.ShapeDtypeStruct(plane + (block, depth), bf16),
        ),
        in_specs=[away] * 5,
        out_specs=(away, away, away),
        scratch_shapes=scratch,
        compiler_params=pltpu.CompilerParams(
            collective_id=0, has_side_effects=True, vmem_limit_bytes=56 * 1024 * 1024
        ),
        cost_estimate=pl.CostEstimate(
            flops=2 * 3 * hidden * depth * tokens,
            bytes_accessed=4 * 3 * hidden * depth,
            transcendentals=0,
        ),
    )(features, cotangent, gate_master, up_master, down_master)
    tile = hidden // 3
    return pl.pallas_call(
        gradients,
        grid=(hidden // tile,),
        out_shape=(
            jax.ShapeDtypeStruct((depth, hidden), bf16),
            jax.ShapeDtypeStruct((depth, hidden), bf16),
            jax.ShapeDtypeStruct((hidden, depth), bf16),
        ),
        in_specs=[
            pl.BlockSpec((depth, tokens), lambda i: (0, 0)),
            pl.BlockSpec((3, tile, tokens), lambda i: (0, i, 0)),
            pl.BlockSpec((tokens, depth), lambda i: (0, 0)),
        ],
        out_specs=(
            pl.BlockSpec((depth, tile), lambda i: (0, i)),
            pl.BlockSpec((depth, tile), lambda i: (0, i)),
            pl.BlockSpec((tile, depth), lambda i: (i, 0)),
        ),
        compiler_params=pltpu.CompilerParams(vmem_limit_bytes=60 * 1024 * 1024),
        cost_estimate=pl.CostEstimate(
            flops=2 * 3 * hidden * depth * tokens,
            bytes_accessed=2 * (5 * hidden * tokens + 3 * hidden * depth),
            transcendentals=0,
        ),
    )(tokens_t, deltas.reshape(3, hidden, tokens), targets.reshape(tokens, depth))


def solution(mesh):
    placed = (
        P(("col", "depth"), "row"),
        P(("col", "depth"), "row"),
        P("row", ("col", "depth")),
        P("row", ("col", "depth")),
        P(("col", "depth"), "row"),
    )
    return jax.shard_map(
        functools.partial(shards, mesh.shape["row"], mesh.shape["col"] // 2, mesh.shape["depth"]),
        mesh=mesh,
        in_specs=placed,
        out_specs=(
            P("row", ("col", "depth")),
            P("row", ("col", "depth")),
            P(("col", "depth"), "row"),
        ),
        check_vma=False,
    )
```
